32 devices in a mesh: groups: 2 (over x), row: 8 (over z, y), col: 2 (over core).
Axes of the slice: x: 2, y: 2, z: 4, core: 2. Of those that a mesh axis runs over, the one named last changes fastest.
Arguments:
- affinity: bfloat16 [4096, 2, 1024], P(('groups', 'col'), None, 'row'), parts along dimension 0, may hold values from 0 to 64, as said below
- block_live: int32 [32, 2, 8], P(('groups', 'col'), None, 'row'), parts along dimension 0, may hold values from 0 to 1, as said below
- labels: bfloat16 [4096, 256], P(('groups', 'col', 'row')), parts along dimension 0, may hold values from 0 to 1
- seed_class: int32 [4096], P(('groups', 'col', 'row')), parts along dimension 0, may hold values from 0 to 149
- seed_mask: int32 [4096], P(('groups', 'col', 'row')), parts along dimension 0, may hold values 0 or 1
Outputs:
- propagated: bfloat16 [4096, 256], P(('groups', 'col', 'row')), parts along dimension 0
The draws below stay inside these ranges and needn't reach their ends.
There are 2 independent parts, one for each index of `groups`. The reference program is written for one: setup_inputs(seed, part) draws one part's arguments, and reference() takes and returns one part's arrays. A program takes and returns all parts, laid end to end along the dimension named above; each array names one. Nothing has to cross between parts.
Inputs may be any that keep to these rules, and one draw needn't show every extreme that they name: `affinity`: positive affinities. `block_live`: 1 where the 128 x 128 block of affinities is stored, 0 where it is absent.
All inputs are finite; a program needn't handle non-finite values. No bound on the sum of `seed_mask` on one device may be relied on, other than what follows from the above.
Results may differ from the reference program's by a relative error of at most 0.0036.
Values may be sent and summed in bfloat16 or wider, within the bound.
No kernel may reach another device: no remote copies, remote signals or barrier semaphores. Data moves between devices by JAX's collectives and lax.ppermute only.
A program may use at most 128 MiB of HBM per device.

```python
import jax
import jax.numpy as jnp
from jax import lax

CLASSES = 256
BLK = 128
NODE_DEV = 128
ITERS = 2
STRIPE = 1024
NODES = 2048


def draw_affinity(key, part):
    key = jax.random.fold_in(key, 11)
    within_key, near_key, row_key, col_key, strong_key = jax.random.split(key, 5)
    shape = (NODES, NODES // STRIPE, STRIPE)
    near_share = 1.0 / 16.0
    near_gain = 40.0
    within = jnp.power(10.0, jax.random.uniform(within_key, shape, jnp.float32, -1.0, 1.0))
    near = jnp.where(jax.random.uniform(near_key, shape, jnp.float32) < near_share, near_gain, 1.0).astype(jnp.float32)
    row_scale = jnp.power(10.0, jax.random.uniform(row_key, (NODES, 1, 1), jnp.float32))
    col_scale = jnp.power(10.0, jax.random.uniform(col_key, (1, NODES // STRIPE, STRIPE), jnp.float32))
    strong = jax.random.randint(strong_key, (NODES // BLK, 1, NODES // STRIPE, STRIPE // BLK, 1), 0, 64)
    boost = jnp.where(strong == 0, 100.0, 1.0).astype(jnp.float32)
    boost = jnp.broadcast_to(boost, (NODES // BLK, BLK, NODES // STRIPE, STRIPE // BLK, BLK)).reshape(shape)
    values = 0.012 / NODES * row_scale * col_scale * within * near * boost
    return values.astype(jnp.bfloat16)


def draw_block_live(key, part):
    key = jax.random.fold_in(key, 23)
    base_key, boost_key, cell_key = jax.random.split(key, 3)
    columns = (1, NODES // STRIPE, STRIPE // BLK)
    level = 2 + jax.random.randint(base_key, columns, 0, 7) * jax.random.randint(boost_key, columns, 0, 2)
    cells = jax.random.randint(cell_key, (NODES // BLK, NODES // STRIPE, STRIPE // BLK), 0, 8)
    return (cells < level).astype(jnp.int32)


def place_ends(result, rng, low, high):
    longest = result.shape.index(max(result.shape))
    spots = []
    for shift in (0, 1):
        where = [jax.random.randint(jax.random.fold_in(rng, axis), (), 0, length) for axis, length in enumerate(result.shape)]
        where[longest] = (where[longest] + shift) % result.shape[longest]
        spots.append(tuple(where))
    return result.at[spots[0]].set(low).at[spots[1]].set(high)


def level_of(key, dims, cuts, smallest, top_value):
    loudness = 1.0
    for dim, parts in cuts:
        draws = jax.random.uniform(jax.random.fold_in(jax.random.fold_in(key, 6), dim), (parts,), jnp.float32, smallest / len(cuts), top_value / len(cuts))
        loudness = loudness * jnp.repeat(jnp.exp(draws), dims[dim] // parts).reshape((-1,) + (1,) * (len(dims) - 1 - dim))
    return loudness


def setup_inputs(seed: int = 0, part: int = 0) -> dict:
    arg_keys = jax.random.split(jax.random.key(seed), 6)
    part_splits = jax.random.split(jax.random.fold_in(arg_keys[5], part), 6)
    affinity = draw_affinity(jax.random.fold_in(jax.random.fold_in(arg_keys[5], part), 71), part)
    block_live = draw_block_live(jax.random.fold_in(jax.random.fold_in(arg_keys[5], part), 71), part)
    labels = jnp.clip(1.0 * jax.random.uniform(part_splits[2], (NODES, CLASSES), jnp.float32) ** level_of(part_splits[2], (NODES, CLASSES), ((0, 16),), -0.2, 0.2), 0.0, 1.0).astype(jnp.bfloat16)
    seed_class = place_ends(jax.random.randint(part_splits[3], (NODES,), 0, 150), jax.random.fold_in(part_splits[3], 1), 0, 149).astype(jnp.int32)
    seed_mask = place_ends((jax.random.randint(part_splits[4], (NODES,), 0, 8) < 1).astype(jnp.int32), jax.random.fold_in(part_splits[4], 1), 0, 1)
    return {"affinity": affinity, "block_live": block_live, "labels": labels, "seed_class": seed_class, "seed_mask": seed_mask}


carry_weight = 0.8


def masked_rows(rows, live_rows):
    shaped = rows.astype(jnp.float32).reshape(live_rows.shape[0], BLK, live_rows.shape[1], BLK)
    keep = (live_rows == 1).astype(jnp.float32)[:, None, :, None]
    return (shaped * keep).reshape(rows.shape[0], rows.shape[1])


def reference(affinity, block_live, labels, seed_class, seed_mask):
    groups_count = NODES // NODE_DEV
    weights = affinity.reshape(groups_count, NODE_DEV, NODES)
    live = block_live.reshape(groups_count, NODE_DEV // BLK, NODES // BLK)

    def degree_step(col_total, item):
        rows, live_rows = item
        matrix = masked_rows(rows, live_rows)
        return col_total + jnp.sum(matrix, axis=0), jnp.sum(matrix, axis=1)

    col_total, row_sums = lax.scan(degree_step, jnp.zeros((NODES,), jnp.float32), (weights, live))
    degree = 1.0 + 0.5 * (row_sums.reshape(NODES) + col_total)

    slots = jnp.arange(CLASSES, dtype=jnp.int32)
    seeds = ((seed_class[:, None] == slots[None, :]) & (seed_mask[:, None] == 1)).astype(jnp.float32)
    current = labels
    for step in range(ITERS):
        dense = current.astype(jnp.float32)
        pieces = dense.reshape(groups_count, NODE_DEV, CLASSES)

        def spread_step(back_total, item):
            rows, live_rows, own_labels = item
            matrix = masked_rows(rows, live_rows)
            forward = jnp.dot(matrix, dense, precision=lax.Precision.HIGHEST)
            backward = jnp.dot(matrix.T, own_labels, precision=lax.Precision.HIGHEST)
            return back_total + backward, forward

        back_total, forward = lax.scan(spread_step, jnp.zeros((NODES, CLASSES), jnp.float32), (weights, live, pieces))
        spread = forward.reshape(NODES, CLASSES) + back_total
        current = (carry_weight * (0.5 * spread + dense) / degree[:, None] + (1.0 - carry_weight) * seeds).astype(jnp.bfloat16)
    return current
```

```python
import jax
import jax.numpy as jnp
from jax import lax
from jax.experimental import pallas as pl
from jax.experimental.pallas import tpu as pltpu
from jax.sharding import PartitionSpec as P

ITERS = 2
CARRY = 0.8
LANES = 128


def gather_rows(own):
    count = lax.axis_size("row")
    pieces = [own]
    for k in range(1, count):
        pieces.append(lax.ppermute(own, "row", [(i, i ^ k) for i in range(count)]))
    return pieces


def swap_cores(value):
    return lax.ppermute(value, "col", [(0, 1), (1, 0)])


def spread_kernel(with_degree, row_ref, here_ref, there_ref, *refs):
    pieces, (keep_ref, give_ref, gathered) = refs[:-3], refs[-3:]
    row, col = row_ref[0], row_ref[1]
    count = len(pieces)
    width, classes = pieces[0].shape
    for k, piece in enumerate(pieces):
        gathered[lax.bitwise_xor(row, k), :, :classes] = piece[...]
    if with_degree:
        gathered[:, :, classes:] = jnp.ones((count, width, LANES), jnp.bfloat16)
    columns = keep_ref.shape[1]

    def side(s):
        def step(r, total):
            values = gathered[r]
            total += lax.dot_general(
                here_ref[r, s], values, (((0,), (0,)), ((), ())), preferred_element_type=jnp.float32
            )
            return total + jnp.dot(there_ref[r, s], values, preferred_element_type=jnp.float32)

        return lax.fori_loop(0, count, step, jnp.zeros((width, columns), jnp.float32), unroll=min(count, 8))

    keep_ref[...] = side(col)
    give_ref[...] = side(1 - col)


def spread_parts(position, here, there, pieces, with_degree):
    width, classes = pieces[0].shape
    columns = classes + (LANES if with_degree else 0)
    count = len(pieces)
    vmem = pl.BlockSpec(memory_space=pltpu.VMEM)
    return pl.pallas_call(
        lambda *refs: spread_kernel(with_degree, *refs),
        out_shape=[jax.ShapeDtypeStruct((width, columns), jnp.float32)] * 2,
        in_specs=[pl.BlockSpec(memory_space=pltpu.SMEM)] + [vmem] * (2 + count),
        out_specs=[vmem, vmem],
        scratch_shapes=[pltpu.VMEM((count, width, columns), jnp.bfloat16)],
        compiler_params=pltpu.CompilerParams(vmem_limit_bytes=40 * 1024 * 1024),
        cost_estimate=pl.CostEstimate(
            flops=8 * count * width * width * columns, bytes_accessed=2 * here.size * 2, transcendentals=0
        ),
    )(position, here, there, *pieces)


def on_device(affinity, block_live, labels, seed_class, seed_mask):
    stripe, sides, width = affinity.shape
    count = stripe // width
    classes = labels.shape[1]
    shaped = affinity.reshape(count, width, sides, width)
    keep = block_live[:, None, :, :] == 1
    stored = jnp.where(keep, shaped, jnp.zeros_like(shaped)).transpose(0, 2, 1, 3)
    mirror = lax.all_to_all(
        stored.reshape(count * sides, width, width), ("row", "col"), split_axis=0, concat_axis=0, tiled=True
    ).reshape(stored.shape)

    slots = lax.broadcasted_iota(jnp.int32, (width, classes), 1)
    is_seed = (seed_class[:, None] == slots) & (seed_mask[:, None] == 1)
    seed_rows = jnp.where(is_seed, 1.0, 0.0).astype(jnp.float32)
    position = jnp.stack([lax.axis_index("row"), lax.axis_index("col")]).astype(jnp.int32)

    current = labels
    degree = None
    for step in range(ITERS):
        pieces = gather_rows(current)
        kept, given = spread_parts(position, stored, mirror, pieces, step == 0)
        spread = kept + swap_cores(given)
        if step == 0:
            degree = 1.0 + 0.5 * spread[:, classes : classes + 1]
            spread = spread[:, :classes]
        mixed = CARRY * (0.5 * spread + current.astype(jnp.float32)) / degree
        current = (mixed + (1.0 - CARRY) * seed_rows).astype(jnp.bfloat16)
    return current


def solution(mesh):
    return jax.shard_map(
        on_device,
        mesh=mesh,
        in_specs=(
            P(("groups", "col"), None, "row"),
            P(("groups", "col"), None, "row"),
            P(("groups", "col", "row"), None),
            P(("groups", "col", "row")),
            P(("groups", "col", "row")),
        ),
        out_specs=P(("groups", "col", "row"), None),
        check_vma=False,
    )
```

```python
import jax
import jax.numpy as jnp
from jax import lax
from jax.experimental import pallas as pl
from jax.experimental.pallas import tpu as pltpu
from jax.sharding import PartitionSpec as P

ITERS = 2
CARRY = 0.8
LANES = 128


def gather_rows(own):
    return lax.all_gather(own, "row", axis=0, tiled=False)


def swap_cores(value):
    return lax.ppermute(value, "col", [(0, 1), (1, 0)])


def spread_kernel(with_degree, col_ref, here_ref, there_ref, values_ref, keep_ref, give_ref):
    col = col_ref[0]
    count, width, classes = values_ref.shape

    def side(s):
        def step(r, totals):
            mirrored = there_ref[r, s]
            total, sums = totals
            values = values_ref[r]
            total += lax.dot_general(
                here_ref[r, s], values, (((0,), (0,)), ((), ())), preferred_element_type=jnp.float32
            )
            total += jnp.dot(mirrored, values, preferred_element_type=jnp.float32)
            if with_degree:
                ones = jnp.ones((width, LANES), jnp.bfloat16)
                sums += lax.dot_general(
                    here_ref[r, s], ones, (((0,), (0,)), ((), ())), preferred_element_type=jnp.float32
                )
                sums += jnp.dot(mirrored, ones, preferred_element_type=jnp.float32)
            return total, sums

        zeros = jnp.zeros((width, classes), jnp.float32), jnp.zeros((width, LANES), jnp.float32)
        return lax.fori_loop(0, count, step, zeros, unroll=min(count, 8))

    for ref, s in ((keep_ref, col), (give_ref, 1 - col)):
        total, sums = side(s)
        ref[:, :classes] = total
        if with_degree:
            ref[:, classes:] = sums


def spread_parts(position, here, there, values, with_degree):
    count, width, classes = values.shape
    columns = classes + (LANES if with_degree else 0)
    vmem = pl.BlockSpec(memory_space=pltpu.VMEM)
    return pl.pallas_call(
        lambda *refs: spread_kernel(with_degree, *refs),
        out_shape=[jax.ShapeDtypeStruct((width, columns), jnp.float32)] * 2,
        in_specs=[pl.BlockSpec(memory_space=pltpu.SMEM)] + [vmem] * 3,
        out_specs=[vmem, vmem],
        compiler_params=pltpu.CompilerParams(vmem_limit_bytes=40 * 1024 * 1024),
        cost_estimate=pl.CostEstimate(
            flops=8 * count * width * width * columns, bytes_accessed=2 * here.size * 2, transcendentals=0
        ),
    )(position, here, there, values)


def on_device(affinity, block_live, labels, seed_class, seed_mask):
    stripe, sides, width = affinity.shape
    count = stripe // width
    classes = labels.shape[1]
    shaped = affinity.reshape(count, width, sides, width)
    keep = block_live[:, None, :, :] == 1
    stored = jnp.where(keep, shaped, jnp.zeros_like(shaped)).transpose(0, 2, 1, 3)
    mirror = lax.all_to_all(
        stored.reshape(count * sides, width, width), ("row", "col"), split_axis=0, concat_axis=0, tiled=True
    ).reshape(stored.shape)

    slots = lax.broadcasted_iota(jnp.int32, (width, classes), 1)
    is_seed = (seed_class[:, None] == slots) & (seed_mask[:, None] == 1)
    seed_rows = jnp.where(is_seed, 1.0, 0.0).astype(jnp.float32)
    position = lax.axis_index("col").astype(jnp.int32).reshape(1)

    current = labels
    degree = None
    for step in range(ITERS):
        values = gather_rows(current)
        kept, given = spread_parts(position, stored, mirror, values, step == 0)
        spread = kept + swap_cores(given)
        if step == 0:
            degree = 1.0 + 0.5 * spread[:, classes : classes + 1]
            spread = spread[:, :classes]
        mixed = CARRY * (0.5 * spread + current.astype(jnp.float32)) / degree
        current = (mixed + (1.0 - CARRY) * seed_rows).astype(jnp.bfloat16)
    return current


def solution(mesh):
    return jax.shard_map(
        on_device,
        mesh=mesh,
        in_specs=(
            P(("groups", "col"), None, "row"),
            P(("groups", "col"), None, "row"),
            P(("groups", "col", "row"), None),
            P(("groups", "col", "row")),
            P(("groups", "col", "row")),
        ),
        out_specs=P(("groups", "col", "row"), None),
        check_vma=False,
    )
```

```python
import jax
import jax.numpy as jnp
from jax import lax
from jax.experimental import pallas as pl
from jax.experimental.pallas import tpu as pltpu
from jax.sharding import PartitionSpec as P

ITERS = 2
CARRY = 0.8
SUBLANES = 8
VMEM_LIMIT = 48 * 1024 * 1024


def split_rows(count):
    inner = 1 << ((count.bit_length() - 1) // 2)
    return count // inner, inner


def swap_rows(value, shift):
    count = lax.axis_size("row")
    return lax.ppermute(value, "row", [(i, i ^ shift) for i in range(count)])


def swap_cores(value):
    return lax.ppermute(value, "col", [(0, 1), (1, 0)])


def call(kernel, out_shape, *operands, smem=0, flops=0):
    spaces = [pltpu.SMEM] * smem + [pltpu.VMEM] * (len(operands) - smem)
    size = sum(x.size * x.dtype.itemsize for x in operands)
    return pl.pallas_call(
        kernel,
        out_shape=out_shape,
        in_specs=[pl.BlockSpec(memory_space=space) for space in spaces],
        out_specs=jax.tree.map(lambda _: pl.BlockSpec(memory_space=pltpu.VMEM), out_shape),
        compiler_params=pltpu.CompilerParams(vmem_limit_bytes=VMEM_LIMIT),
        cost_estimate=pl.CostEstimate(flops=flops, bytes_accessed=size, transcendentals=0),
    )(*operands)


def prepare_kernel(z_count, y_count, place, live, tile, *outs):
    z, y, col = place[0], place[1], place[2]
    own_side, other_side, halves = outs[0], outs[1], outs[2:]
    width = tile.shape[1]
    out_row = lax.broadcasted_iota(jnp.int32, (2 * width, 2 * width), 0)
    in_row = lax.broadcasted_iota(jnp.int32, (2 * width, 2 * width), 1)
    side = lax.bitwise_xor((out_row >= width).astype(jnp.int32), col)
    spot = 2 * lax.rem(out_row, width) + side
    sort = jnp.where(in_row == spot, 1.0, 0.0).astype(jnp.bfloat16)
    for k in range(z_count):
        for j in range(y_count):
            block = lax.bitwise_xor(z, k) * y_count + lax.bitwise_xor(y, j)
            rows = tile[pl.ds(pl.multiple_of(block * 2 * width, 2 * width), 2 * width), :]
            sides = jnp.dot(sort, rows, preferred_element_type=jnp.float32)
            for i in range(2):
                keep = live[block, lax.bitwise_xor(col, i)] == 1
                piece = sides[i * width : (i + 1) * width]
                piece = jnp.where(keep, piece, jnp.zeros_like(piece)).astype(jnp.bfloat16)
                (own_side, other_side)[i][k, j] = piece
                halves[j][i, k] = piece


def merge_kernel(own_side, from_core, *outs):
    for k, out in enumerate(outs):
        out[0] = own_side[k + 1]
        out[1] = from_core[k + 1]


def spread_kernel(z_count, y_count, with_degree, *refs):
    halves, refs = refs[:y_count], refs[y_count:]
    own_side, from_core, refs = refs[0], refs[1], refs[2:]
    strips, refs = refs[: z_count - 1], refs[z_count - 1 :]
    pieces, refs = refs[:z_count], refs[z_count:]
    keeps, give = refs[:-1], refs[-1]
    values = jnp.concatenate([piece[...] for piece in pieces], axis=0)
    depth, classes = values.shape
    width = depth // z_count
    ones = jnp.ones((SUBLANES, depth), jnp.bfloat16)

    def strip(k, i, j):
        if k > 0:
            return strips[k - 1][i, j]
        return (own_side, from_core)[i][0, j]

    for i in range(2):
        for j in range(y_count):
            back = halves[j][i].reshape(depth, width)
            ahead = jnp.concatenate([strip(k, i, j) for k in range(z_count)], axis=1)
            total = lax.dot_general(back, values, (((0,), (0,)), ((), ())), preferred_element_type=jnp.float32)
            total += jnp.dot(ahead, values, preferred_element_type=jnp.float32)
            out = keeps[j] if i == 0 else give.at[j]
            out[:width, :] = total
            if with_degree:
                sums = jnp.dot(ones, back, preferred_element_type=jnp.float32)
                sums += lax.dot_general(ones, ahead, (((1,), (1,)), ((), ())), preferred_element_type=jnp.float32)
                out[width:, :] = jnp.concatenate([sums] * (classes // width), axis=1)


def on_device(affinity, block_live, labels, seed_class, seed_mask):
    stripe, sides, width = affinity.shape
    count = lax.axis_size("row")
    z_count, y_count = split_rows(count)
    classes = labels.shape[1]
    row = lax.axis_index("row").astype(jnp.int32)
    col = lax.axis_index("col").astype(jnp.int32)
    place = jnp.stack([row // y_count, row % y_count, col])

    blocks = jax.ShapeDtypeStruct((z_count, y_count, width, width), jnp.bfloat16)
    half = jax.ShapeDtypeStruct((2, z_count, width, width), jnp.bfloat16)
    own_side, other_side, *halves = call(
        lambda *refs: prepare_kernel(z_count, y_count, *refs),
        [blocks, blocks] + [half] * y_count,
        place,
        block_live.reshape(count, sides),
        affinity.reshape(stripe * sides, width),
        smem=2,
        flops=2 * 2 * stripe * width * 2 * width,
    )
    from_core = swap_cores(other_side)
    halves = [halves[0]] + [swap_rows(halves[j], j) for j in range(1, y_count)]
    strip = jax.ShapeDtypeStruct((2, y_count, width, width), jnp.bfloat16)
    strips = call(merge_kernel, [strip] * (z_count - 1), own_side, from_core)
    strips = [swap_rows(piece, (k + 1) * y_count) for k, piece in enumerate(strips)]

    slots = lax.broadcasted_iota(jnp.int32, (width, classes), 1)
    is_seed = (seed_class[:, None] == slots) & (seed_mask[:, None] == 1)
    seed_rows = jnp.where(is_seed, 1.0, 0.0).astype(jnp.float32)

    current = labels
    degree = None
    for step in range(ITERS):
        pieces = [current] + [swap_rows(current, k * y_count) for k in range(1, z_count)]
        height = width + (SUBLANES if step == 0 else 0)
        part = jax.ShapeDtypeStruct((height, classes), jnp.float32)
        parts = jax.ShapeDtypeStruct((y_count, height, classes), jnp.float32)
        *keeps, give = call(
            lambda *refs: spread_kernel(z_count, y_count, step == 0, *refs),
            [part] * y_count + [parts],
            *halves,
            own_side,
            from_core,
            *strips,
            *pieces,
            flops=2 * 2 * 2 * y_count * z_count * width * width * classes,
        )
        taken = swap_cores(give)
        spread = keeps[0] + taken[0]
        for j in range(1, y_count):
            spread = spread + swap_rows(keeps[j] + taken[j], j)
        if step == 0:
            degree = 1.0 + 0.5 * spread[width, :width][:, None]
        mixed = CARRY * (0.5 * spread[:width] + current.astype(jnp.float32)) / degree
        current = (mixed + (1.0 - CARRY) * seed_rows).astype(jnp.bfloat16)
    return current


def solution(mesh):
    return jax.shard_map(
        on_device,
        mesh=mesh,
        in_specs=(
            P(("groups", "col"), None, "row"),
            P(("groups", "col"), None, "row"),
            P(("groups", "col", "row"), None),
            P(("groups", "col", "row")),
            P(("groups", "col", "row")),
        ),
        out_specs=P(("groups", "col", "row"), None),
        check_vma=False,
    )
```

```python
import jax
import jax.numpy as jnp
from jax import lax
from jax.experimental import pallas as pl
from jax.experimental.pallas import tpu as pltpu
from jax.sharding import PartitionSpec as P

ITERS = 2
CARRY = 0.8
SUBLANES = 8
VMEM_LIMIT = 48 * 1024 * 1024


def split_rows(count):
    inner = 1 << ((count.bit_length() - 1) // 2)
    return count // inner, inner


def swap_rows(value, shift):
    count = lax.axis_size("row")
    return lax.ppermute(value, "row", [(i, i ^ shift) for i in range(count)])


def swap_cores(value):
    return lax.ppermute(value, "col", [(0, 1), (1, 0)])


def call(kernel, out_shape, *operands, smem=0, flops=0):
    spaces = [pltpu.SMEM] * smem + [pltpu.VMEM] * (len(operands) - smem)
    size = sum(x.size * x.dtype.itemsize for x in operands)
    return pl.pallas_call(
        kernel,
        out_shape=out_shape,
        in_specs=[pl.BlockSpec(memory_space=space) for space in spaces],
        out_specs=jax.tree.map(lambda _: pl.BlockSpec(memory_space=pltpu.VMEM), out_shape),
        compiler_params=pltpu.CompilerParams(vmem_limit_bytes=VMEM_LIMIT),
        cost_estimate=pl.CostEstimate(flops=flops, bytes_accessed=size, transcendentals=0),
    )(*operands)


def far_first(count):
    half = count // 2
    return [k for k in range(half, count)] + [k for k in range(1, half)]


def prepare_kernel(z_count, y_count, live, tile_hbm, own_side, other_side, tile, arrived):
    row, col = lax.axis_index("row"), lax.axis_index("col")
    z, y = lax.div(row, y_count), lax.rem(row, y_count)
    width = tile_hbm.shape[1]
    span = 2 * y_count * width

    def fetch(k):
        start = pl.multiple_of(lax.bitwise_xor(z, k) * span, span)
        return pltpu.make_async_copy(tile_hbm.at[pl.ds(start, span)], tile.at[k], arrived.at[k])

    for k in range(z_count):
        fetch(k).start()
    out_row = lax.broadcasted_iota(jnp.int32, (2 * width, 2 * width), 0)
    in_row = lax.broadcasted_iota(jnp.int32, (2 * width, 2 * width), 1)
    side = lax.bitwise_xor((out_row >= width).astype(jnp.int32), col)
    spot = 2 * lax.rem(out_row, width) + side
    sort = jnp.where(in_row == spot, 1.0, 0.0).astype(jnp.bfloat16)
    for k in range(z_count):
        fetch(k).wait()
        for j in range(y_count):
            near = lax.bitwise_xor(y, j)
            block = lax.bitwise_xor(z, k) * y_count + near
            rows = tile[k, pl.ds(pl.multiple_of(near * 2 * width, 2 * width), 2 * width), :]
            sides = jnp.dot(sort, rows, preferred_element_type=jnp.float32)
            for i, out in enumerate((own_side, other_side)):
                keep = live[lax.bitwise_xor(col, i), 0, block] == 1
                piece = sides[i * width : (i + 1) * width]
                out[k, j] = jnp.where(keep, piece, jnp.zeros_like(piece)).astype(jnp.bfloat16)


def merge_kernel(z_count, y_count, own_side, other_side, from_core, own, far, seed_class, seed_mask, *outs):
    strips, halves, (pair, base) = outs[: z_count - 1], outs[z_count - 1 : -2], outs[-2:]
    for k, out in zip(far_first(z_count), strips):
        out[0] = own_side[k]
        out[1] = from_core[k]
    for j, out in enumerate(halves):
        out[0] = own_side[:, j + 1]
        out[1] = other_side[:, j + 1]
    width, classes = own.shape
    pair[:width] = own[...]
    pair[width:] = far[...]
    kind = jnp.where(seed_mask[...] == 1, seed_class[...], -1)
    kind = jnp.transpose(jnp.broadcast_to(kind, (width, width)))
    for start in range(0, classes, width):
        slots = lax.broadcasted_iota(jnp.int32, (width, width), 1) + start
        base[:, start : start + width] = jnp.where(kind == slots, 1.0 - CARRY, 0.0)


def spread_kernel(order, y_count, with_degree, *refs):
    z_count = len(order)
    own_side, other_side, from_core, refs = refs[0], refs[1], refs[2], refs[3:]
    strips, refs = dict(zip(far_first(z_count), refs)), refs[z_count - 1 :]
    halves, refs = refs[: y_count - 1], refs[y_count - 1 :]
    pieces, keeps, give = refs[: -y_count - 1], refs[-y_count - 1 : -1], refs[-1]
    values = jnp.concatenate([piece[...] for piece in pieces], axis=0)
    depth, classes = values.shape
    width = depth // z_count
    ones = jnp.ones((SUBLANES, depth), jnp.bfloat16)

    def back_block(k, i, j):
        if j > 0:
            return halves[j - 1][i, k]
        return (own_side, other_side)[i][k, 0]

    def ahead_block(k, i, j):
        if k > 0:
            return strips[k][i, j]
        return (own_side, from_core)[i][0, j]

    for i in (1, 0):
        for j in range(y_count):
            back = jnp.concatenate([back_block(k, i, j) for k in order], axis=0)
            ahead = jnp.concatenate([ahead_block(k, i, j) for k in order], axis=1)
            total = lax.dot_general(back, values, (((0,), (0,)), ((), ())), preferred_element_type=jnp.float32)
            total += jnp.dot(ahead, values, preferred_element_type=jnp.float32)
            out = keeps[j] if i == 0 else give.at[j]
            out[:width, :] = total
            if with_degree:
                sums = jnp.dot(ones, back, preferred_element_type=jnp.float32)
                sums += lax.dot_general(ones, ahead, (((1,), (1,)), ((), ())), preferred_element_type=jnp.float32)
                out[width:, :] = jnp.concatenate([sums] * (classes // width), axis=1)


def on_device(affinity, block_live, labels, seed_class, seed_mask):
    stripe, sides, width = affinity.shape
    count = lax.axis_size("row")
    z_count, y_count = split_rows(count)
    classes = labels.shape[1]

    blocks = jax.ShapeDtypeStruct((z_count, y_count, width, width), jnp.bfloat16)
    own_side, other_side = pl.pallas_call(
        lambda *refs: prepare_kernel(z_count, y_count, *refs),
        out_shape=[blocks, blocks],
        in_specs=[pl.BlockSpec(memory_space=pltpu.SMEM), pl.BlockSpec(memory_space=pltpu.HBM)],
        out_specs=[pl.BlockSpec(memory_space=pltpu.VMEM)] * 2,
        scratch_shapes=[
            pltpu.VMEM((z_count, 2 * y_count * width, width), jnp.bfloat16),
            pltpu.SemaphoreType.DMA((z_count,)),
        ],
        compiler_params=pltpu.CompilerParams(vmem_limit_bytes=VMEM_LIMIT),
    )(block_live.transpose(1, 2, 0), affinity.reshape(stripe * sides, width))
    from_core = swap_cores(other_side)
    far = swap_rows(labels, (z_count // 2) * y_count)

    strip = jax.ShapeDtypeStruct((2, y_count, width, width), jnp.bfloat16)
    half = jax.ShapeDtypeStruct((2, z_count, width, width), jnp.bfloat16)
    pair = jax.ShapeDtypeStruct((2 * width, classes), jnp.bfloat16)
    base = jax.ShapeDtypeStruct((width, classes), jnp.float32)
    merged = call(
        lambda *refs: merge_kernel(z_count, y_count, *refs),
        [strip] * (z_count - 1) + [half] * (y_count - 1) + [pair, base],
        own_side,
        other_side,
        from_core,
        labels,
        far,
        seed_class.reshape(1, width),
        seed_mask.reshape(1, width),
    )
    base = merged[-1]
    strips = [swap_rows(x, k * y_count) for k, x in zip(far_first(z_count), merged)]
    halves = [swap_rows(x, j + 1) for j, x in enumerate(merged[z_count - 1 : -2])]
    values, order, bit = merged[-2], [0, z_count // 2], z_count // 4
    pieces = [values]
    while bit:
        pieces.append(swap_rows(values, bit * y_count))
        order = order + [k ^ bit for k in order]
        bit //= 2
        if bit:
            values = jnp.concatenate(pieces, axis=0)
            pieces = [values]

    current = labels
    degree = None
    for step in range(ITERS):
        if step > 0:
            order = [0] + far_first(z_count)
            pieces = [current] + [swap_rows(current, k * y_count) for k in order[1:]]
        height = width + (SUBLANES if step == 0 else 0)
        part = jax.ShapeDtypeStruct((height, classes), jnp.float32)
        parts = jax.ShapeDtypeStruct((y_count, height, classes), jnp.float32)
        *keeps, give = call(
            lambda *refs: spread_kernel(order, y_count, step == 0, *refs),
            [part] * y_count + [parts],
            own_side,
            other_side,
            from_core,
            *strips,
            *halves,
            *pieces,
            flops=2 * 2 * 2 * y_count * z_count * width * width * classes,
        )
        taken = swap_cores(give)
        spread = keeps[0] + taken[0]
        for j in range(1, y_count):
            spread = spread + swap_rows(keeps[j] + taken[j], j)
        if step == 0:
            degree = 1.0 + 0.5 * spread[width, :width][:, None]
        mixed = CARRY * (0.5 * spread[:width] + current.astype(jnp.float32)) / degree
        current = (mixed + base).astype(jnp.bfloat16)
    return current


def solution(mesh):
    return jax.shard_map(
        on_device,
        mesh=mesh,
        in_specs=(
            P(("groups", "col"), None, "row"),
            P(("groups", "col"), None, "row"),
            P(("groups", "col", "row"), None),
            P(("groups", "col", "row")),
            P(("groups", "col", "row")),
        ),
        out_specs=P(("groups", "col", "row"), None),
        check_vma=False,
    )
```

```python
import jax
import jax.numpy as jnp
from jax import lax
from jax.experimental import pallas as pl
from jax.experimental.pallas import tpu as pltpu
from jax.sharding import PartitionSpec as P

ITERS = 2
CARRY = 0.8
SUBLANES = 8
JOIN_FLOPS = 0
SIDES_FLOPS = 3_000_000_000
MIB = 1024 * 1024


def split_rows(count):
    inner = 1 << ((count.bit_length() - 1) // 2)
    return count // inner, inner


def swap_rows(value, shift):
    count = lax.axis_size("row")
    return lax.ppermute(value, "row", [(i, i ^ shift) for i in range(count)])


def swap_cores(value):
    return lax.ppermute(value, "col", [(0, 1), (1, 0)])


def call(kernel, out_shape, *operands, smem=0, flops=0):
    spaces = [pltpu.SMEM] * smem + [pltpu.VMEM] * (len(operands) - smem)
    size = sum(x.size * x.dtype.itemsize for x in (*operands, *jax.tree.leaves(out_shape)))
    return pl.pallas_call(
        kernel,
        out_shape=out_shape,
        in_specs=[pl.BlockSpec(memory_space=space) for space in spaces],
        out_specs=jax.tree.map(lambda _: pl.BlockSpec(memory_space=pltpu.VMEM), out_shape),
        compiler_params=pltpu.CompilerParams(vmem_limit_bytes=2 * size + 4 * MIB),
        cost_estimate=pl.CostEstimate(flops=flops, bytes_accessed=size, transcendentals=0),
    )(*operands)


def far_first(count):
    half = count // 2
    return [k for k in range(half, count)] + [k for k in range(1, half)]


def prepare_kernel(z_count, y_count, live, tile, *outs):
    strips, halves = outs[:z_count], outs[z_count:]
    row, col = lax.axis_index("row"), lax.axis_index("col")
    z, y = lax.div(row, y_count), lax.rem(row, y_count)
    width = tile.shape[1]
    out_row = lax.broadcasted_iota(jnp.int32, (2 * width, 2 * width), 0)
    in_row = lax.broadcasted_iota(jnp.int32, (2 * width, 2 * width), 1)
    side = lax.bitwise_xor((out_row >= width).astype(jnp.int32), col)
    spot = 2 * lax.rem(out_row, width) + side
    sort = jnp.where(in_row == spot, 1.0, 0.0).astype(jnp.bfloat16)
    for k in range(z_count):
        for j in range(y_count):
            block = lax.bitwise_xor(z, k) * y_count + lax.bitwise_xor(y, j)
            rows = tile[pl.ds(pl.multiple_of(block * 2 * width, 2 * width), 2 * width), :]
            sides = jnp.dot(sort, rows, preferred_element_type=jnp.float32)
            for i in range(2):
                keep = live[lax.bitwise_xor(col, i), 0, block] == 1
                piece = sides[i * width : (i + 1) * width]
                piece = jnp.where(keep, piece, jnp.zeros_like(piece)).astype(jnp.bfloat16)
                strips[k][i, j] = piece
                if j > 0:
                    halves[j - 1][i, k] = piece


def join_kernel(*refs):
    parts, out = refs[:-1], refs[-1]
    start = 0
    for part in parts:
        out[start : start + part.shape[0]] = part[...]
        start += part.shape[0]


def join(parts, flops=0):
    rows = sum(x.shape[0] for x in parts)
    return call(join_kernel, jax.ShapeDtypeStruct((rows,) + parts[0].shape[1:], parts[0].dtype), *parts, flops=flops)


def other_kernel(*refs):
    strips, out = refs[:-1], refs[-1]
    for k, strip in zip([0] + far_first(len(strips)), strips):
        out[k] = strip[1]


def seed_kernel(seed_class, seed_mask, base):
    width, classes = base.shape
    kind = jnp.where(seed_mask[...] == 1, seed_class[...], -1)
    kind = jnp.transpose(jnp.broadcast_to(kind, (width, width)))
    for start in range(0, classes, width):
        slots = lax.broadcasted_iota(jnp.int32, (width, width), 1) + start
        base[:, start : start + width] = jnp.where(kind == slots, 1.0 - CARRY, 0.0)


def spread_kernel(order, y_count, first, *refs):
    z_count = len(order)
    sent, refs = refs[:z_count], refs[z_count:]
    strips = dict(zip([0] + far_first(z_count), sent[:1] + refs))
    refs = refs[z_count - 1 :]
    halves, refs = refs[: y_count - 1], refs[y_count - 1 :]
    other, refs = refs[0], refs[1:]
    pieces, keeps, give = refs[: -y_count - 1], refs[-y_count - 1 : -1], refs[-1]
    if first:
        pieces, theirs = pieces[: len(pieces) // 2], pieces[len(pieces) // 2 :]
        theirs = jnp.concatenate([piece[...] for piece in theirs], axis=0)
    values = jnp.concatenate([piece[...] for piece in pieces], axis=0)
    depth, classes = values.shape
    width = depth // z_count
    ones = jnp.ones((SUBLANES, depth), jnp.bfloat16)

    def product(left, right, contract):
        return lax.dot_general(left, right, ((contract[:1], contract[1:]), ((), ())), preferred_element_type=jnp.float32)

    for i in (1, 0):
        for j in range(y_count):
            back = jnp.concatenate([sent[k][i, 0] if j == 0 else halves[j - 1][i, k] for k in order], axis=0)
            total = product(back, values, (0, 0))
            ahead = []
            if first and i == 0:
                ahead = [(0, values), (1, theirs)]
                ahead = [(jnp.concatenate([strips[k][s, j] for k in order], axis=1), v) for s, v in ahead]
            elif not first:
                ahead = [strips[k][0, j] if i == 0 else other[k, j] for k in order]
                ahead = [(jnp.concatenate(ahead, axis=1), values)]
            for blocks, right in ahead:
                total += product(blocks, right, (1, 0))
            out = keeps[j] if i == 0 else give.at[j]
            out[:width, :] = total
            if first:
                sums = product(ones, back, (1, 0))
                for blocks, _ in ahead:
                    sums += product(ones, blocks, (1, 1))
                out[width:, :] = jnp.concatenate([sums] * (classes // width), axis=1)


def on_device(affinity, block_live, labels, seed_class, seed_mask):
    stripe, sides, width = affinity.shape
    count = lax.axis_size("row")
    z_count, y_count = split_rows(count)
    classes = labels.shape[1]

    strip = jax.ShapeDtypeStruct((2, y_count, width, width), jnp.bfloat16)
    half = jax.ShapeDtypeStruct((2, z_count, width, width), jnp.bfloat16)
    sent = call(
        lambda *refs: prepare_kernel(z_count, y_count, *refs),
        [strip] * z_count + [half] * (y_count - 1),
        block_live.transpose(1, 2, 0),
        affinity.reshape(stripe * sides, width),
        smem=1,
    )
    sent, halves = sent[:z_count], sent[z_count:]
    arrived = {k: swap_rows(sent[k], k * y_count) for k in far_first(z_count)}
    strips = [arrived[k] for k in far_first(z_count)]
    halves = [swap_rows(x, j + 1) for j, x in enumerate(halves)]
    near = {k: swap_rows(labels, k * y_count) for k in far_first(z_count) if k & (k - 1) == 0}
    for k in far_first(z_count):
        if k not in near:
            low = k & -k
            near[k] = swap_rows(near[k ^ low], low * y_count)
    order = [0] + sorted(near, key=lambda k: (k & (k - 1) != 0, -k))
    values = join([labels] + [near[k] for k in order[1:]], flops=JOIN_FLOPS)
    swapped = swap_cores(values)
    other = jax.ShapeDtypeStruct((z_count, y_count, width, width), jnp.bfloat16)
    sides = call(other_kernel, other, sent[0], *strips, flops=SIDES_FLOPS)
    other = swap_cores(sides)
    pieces = [sides, values, swapped]
    base = call(
        seed_kernel,
        jax.ShapeDtypeStruct((width, classes), jnp.float32),
        seed_class.reshape(1, width),
        seed_mask.reshape(1, width),
    )

    current = labels
    degree = None
    for step in range(ITERS):
        if step > 0:
            order = [0] + far_first(z_count)
            pieces = [other, current] + [swap_rows(current, k * y_count) for k in order[1:]]
        height = width + (SUBLANES if step == 0 else 0)
        part = jax.ShapeDtypeStruct((height, classes), jnp.float32)
        parts = jax.ShapeDtypeStruct((y_count, height, classes), jnp.float32)
        *keeps, give = call(
            lambda *refs: spread_kernel(order, y_count, step == 0, *refs),
            [part] * y_count + [parts],
            *sent,
            *strips,
            *halves,
            *pieces,
            flops=2 * 2 * 2 * y_count * z_count * width * width * classes,
        )
        taken = swap_cores(give)
        spread = keeps[0] + taken[0]
        for j in range(1, y_count):
            spread = spread + swap_rows(keeps[j] + taken[j], j)
        if step == 0:
            degree = 1.0 + 0.5 * spread[width, :width][:, None]
        mixed = CARRY * (0.5 * spread[:width] + current.astype(jnp.float32)) / degree
        current = (mixed + base).astype(jnp.bfloat16)
    return current


def solution(mesh):
    return jax.shard_map(
        on_device,
        mesh=mesh,
        in_specs=(
            P(("groups", "col"), None, "row"),
            P(("groups", "col"), None, "row"),
            P(("groups", "col", "row"), None),
            P(("groups", "col", "row")),
            P(("groups", "col", "row")),
        ),
        out_specs=P(("groups", "col", "row"), None),
        check_vma=False,
    )
```

```python
import jax
import jax.numpy as jnp
from jax import lax
from jax.experimental import pallas as pl
from jax.experimental.pallas import tpu as pltpu
from jax.sharding import PartitionSpec as P

ITERS = 2
CARRY = 0.8
SUBLANES = 8
JOIN_FLOPS = 3_000_000_000
SIDES_FLOPS = 2_000_000_000
MIB = 1024 * 1024


def split_rows(count):
    inner = 1 << ((count.bit_length() - 1) // 2)
    return count // inner, inner


def swap_rows(value, shift):
    count = lax.axis_size("row")
    return lax.ppermute(value, "row", [(i, i ^ shift) for i in range(count)])


def swap_cores(value):
    return lax.ppermute(value, "col", [(0, 1), (1, 0)])


def call(kernel, out_shape, *operands, smem=0, flops=0):
    spaces = [pltpu.SMEM] * smem + [pltpu.VMEM] * (len(operands) - smem)
    size = sum(x.size * x.dtype.itemsize for x in (*operands, *jax.tree.leaves(out_shape)))
    return pl.pallas_call(
        kernel,
        out_shape=out_shape,
        in_specs=[pl.BlockSpec(memory_space=space) for space in spaces],
        out_specs=jax.tree.map(lambda _: pl.BlockSpec(memory_space=pltpu.VMEM), out_shape),
        compiler_params=pltpu.CompilerParams(vmem_limit_bytes=2 * size + 4 * MIB),
        cost_estimate=pl.CostEstimate(flops=flops, bytes_accessed=size, transcendentals=0),
    )(*operands)


def far_first(count):
    half = count // 2
    return [k for k in range(half, count)] + [k for k in range(1, half)]


def prepare_kernel(z_count, y_count, live, tile, *outs):
    strips, halves = outs[:z_count], outs[z_count:]
    row, col = lax.axis_index("row"), lax.axis_index("col")
    z, y = lax.div(row, y_count), lax.rem(row, y_count)
    width = tile.shape[1]
    out_row = lax.broadcasted_iota(jnp.int32, (2 * width, 2 * width), 0)
    in_row = lax.broadcasted_iota(jnp.int32, (2 * width, 2 * width), 1)
    side = lax.bitwise_xor((out_row >= width).astype(jnp.int32), col)
    spot = 2 * lax.rem(out_row, width) + side
    sort = jnp.where(in_row == spot, 1.0, 0.0).astype(jnp.bfloat16)
    for k in range(z_count):
        for j in range(y_count):
            block = lax.bitwise_xor(z, k) * y_count + lax.bitwise_xor(y, j)
            rows = tile[pl.ds(pl.multiple_of(block * 2 * width, 2 * width), 2 * width), :]
            sides = jnp.dot(sort, rows, preferred_element_type=jnp.float32)
            for i in range(2):
                keep = live[lax.bitwise_xor(col, i), 0, block] == 1
                piece = sides[i * width : (i + 1) * width]
                piece = jnp.where(keep, piece, jnp.zeros_like(piece)).astype(jnp.bfloat16)
                strips[k][i, j] = piece
                if j > 0:
                    halves[j - 1][i, k] = piece


def fold_kernel(y_count, first, *refs):
    keeps, taken, (total, *sends) = refs[:y_count], refs[y_count], refs[y_count + 1 :]
    total[...] = keeps[0][...] + taken[0]
    for j, send in enumerate(sends, 1):
        both = keeps[j][...] + taken[j]
        width = both.shape[0] - (SUBLANES if first else 0)
        send[:width, :] = both[:width].astype(jnp.bfloat16)
        if first:
            sums = jnp.concatenate([both[width:]] * 2, axis=0)
            high = sums.astype(jnp.bfloat16).astype(jnp.float32)
            middle = (sums - high).astype(jnp.bfloat16).astype(jnp.float32)
            row = lax.broadcasted_iota(jnp.int32, sums.shape, 0)
            terms = jnp.where(row == 0, high, jnp.where(row == 1, middle, sums - high - middle))
            send[width:, :] = terms.astype(jnp.bfloat16)


def join_kernel(*refs):
    parts, out = refs[:-1], refs[-1]
    start = 0
    for part in parts:
        out[start : start + part.shape[0]] = part[...]
        start += part.shape[0]


def join(parts, flops=0):
    rows = sum(x.shape[0] for x in parts)
    return call(join_kernel, jax.ShapeDtypeStruct((rows,) + parts[0].shape[1:], parts[0].dtype), *parts, flops=flops)


def other_kernel(*refs):
    strips, out = refs[:-1], refs[-1]
    for k, strip in zip([0] + far_first(len(strips)), strips):
        out[k] = strip[1]


def seed_kernel(seed_class, seed_mask, base):
    width, classes = base.shape
    kind = jnp.where(seed_mask[...] == 1, seed_class[...], -1)
    kind = jnp.transpose(jnp.broadcast_to(kind, (width, width)))
    for start in range(0, classes, width):
        slots = lax.broadcasted_iota(jnp.int32, (width, width), 1) + start
        base[:, start : start + width] = jnp.where(kind == slots, 1.0 - CARRY, 0.0)


def spread_kernel(order, y_count, first, *refs):
    z_count = len(order)
    sent, refs = refs[:z_count], refs[z_count:]
    strips = dict(zip([0] + far_first(z_count), sent[:1] + refs))
    refs = refs[z_count - 1 :]
    halves, refs = refs[: y_count - 1], refs[y_count - 1 :]
    other, refs = refs[0], refs[1:]
    pieces, keeps, give = refs[: -y_count - 1], refs[-y_count - 1 : -1], refs[-1]
    if first:
        pieces, theirs = pieces[: len(pieces) // 2], pieces[len(pieces) // 2 :]
        theirs = jnp.concatenate([piece[...] for piece in theirs], axis=0)
    values = jnp.concatenate([piece[...] for piece in pieces], axis=0)
    depth, classes = values.shape
    width = depth // z_count
    ones = jnp.ones((SUBLANES, depth), jnp.bfloat16)

    def product(left, right, contract):
        return lax.dot_general(left, right, ((contract[:1], contract[1:]), ((), ())), preferred_element_type=jnp.float32)

    for i in (1, 0):
        for j in range(y_count):
            back = jnp.concatenate([sent[k][i, 0] if j == 0 else halves[j - 1][i, k] for k in order], axis=0)
            total = product(back, values, (0, 0))
            ahead = []
            if first and i == 0:
                ahead = [(0, values), (1, theirs)]
                ahead = [(jnp.concatenate([strips[k][s, j] for k in order], axis=1), v) for s, v in ahead]
            elif not first:
                ahead = [strips[k][0, j] if i == 0 else other[k, j] for k in order]
                ahead = [(jnp.concatenate(ahead, axis=1), values)]
            for blocks, right in ahead:
                total += product(blocks, right, (1, 0))
            out = keeps[j] if i == 0 else give.at[j]
            out[:width, :] = total
            if first:
                sums = product(ones, back, (1, 0))
                for blocks, _ in ahead:
                    sums += product(ones, blocks, (1, 1))
                out[width:, :] = jnp.concatenate([sums] * (classes // width), axis=1)


def on_device(affinity, block_live, labels, seed_class, seed_mask):
    stripe, sides, width = affinity.shape
    count = lax.axis_size("row")
    z_count, y_count = split_rows(count)
    classes = labels.shape[1]

    strip = jax.ShapeDtypeStruct((2, y_count, width, width), jnp.bfloat16)
    half = jax.ShapeDtypeStruct((2, z_count, width, width), jnp.bfloat16)
    sent = call(
        lambda *refs: prepare_kernel(z_count, y_count, *refs),
        [strip] * z_count + [half] * (y_count - 1),
        block_live.transpose(1, 2, 0),
        affinity.reshape(stripe * sides, width),
        smem=1,
    )
    sent, halves = list(sent[:z_count]), sent[z_count:]
    current, sent[0] = lax.optimization_barrier((labels, sent[0]))
    arrived = {k: swap_rows(sent[k], k * y_count) for k in far_first(z_count)}
    strips = [arrived[k] for k in far_first(z_count)]
    halves = [swap_rows(x, j + 1) for j, x in enumerate(halves)]
    order = [0] + far_first(z_count)
    values = join([current] + [swap_rows(current, k * y_count) for k in order[1:]], flops=JOIN_FLOPS)
    swapped = swap_cores(values)
    other = jax.ShapeDtypeStruct((z_count, y_count, width, width), jnp.bfloat16)
    sides = call(other_kernel, other, sent[0], *strips, flops=SIDES_FLOPS)
    other = swap_cores(sides)
    pieces = [sides, values, swapped]
    base = call(
        seed_kernel,
        jax.ShapeDtypeStruct((width, classes), jnp.float32),
        seed_class.reshape(1, width),
        seed_mask.reshape(1, width),
    )

    degree = None
    for step in range(ITERS):
        if step > 0:
            pieces = [other, current] + [swap_rows(current, k * y_count) for k in order[1:]]
        height = width + (SUBLANES if step == 0 else 0)
        part = jax.ShapeDtypeStruct((height, classes), jnp.float32)
        parts = jax.ShapeDtypeStruct((y_count, height, classes), jnp.float32)
        *keeps, give = call(
            lambda *refs: spread_kernel(order, y_count, step == 0, *refs),
            [part] * y_count + [parts],
            *sent,
            *strips,
            *halves,
            *pieces,
            flops=2 * 2 * 2 * y_count * z_count * width * width * classes,
        )
        taken = swap_cores(give)
        send = jax.ShapeDtypeStruct((width + (2 * SUBLANES if step == 0 else 0), classes), jnp.bfloat16)
        total, *sends = call(
            lambda *refs: fold_kernel(y_count, step == 0, *refs), [part] + [send] * (y_count - 1), *keeps, taken
        )
        sends = [swap_rows(x, j + 1).astype(jnp.float32) for j, x in enumerate(sends)]
        spread = sum((x[:width] for x in sends), total[:width])
        if step == 0:
            sums = sum((x[width : width + 3, :width].sum(axis=0) for x in sends), total[width, :width])
            degree = 1.0 + 0.5 * sums[:, None]
        mixed = CARRY * (0.5 * spread + current.astype(jnp.float32)) / degree
        current = (mixed + base).astype(jnp.bfloat16)
    return current


def solution(mesh):
    return jax.shard_map(
        on_device,
        mesh=mesh,
        in_specs=(
            P(("groups", "col"), None, "row"),
            P(("groups", "col"), None, "row"),
            P(("groups", "col", "row"), None),
            P(("groups", "col", "row")),
            P(("groups", "col", "row")),
        ),
        out_specs=P(("groups", "col", "row"), None),
        check_vma=False,
    )
```

```python
import jax
import jax.numpy as jnp
from jax import lax
from jax.experimental import pallas as pl
from jax.experimental.pallas import tpu as pltpu
from jax.sharding import PartitionSpec as P

ITERS = 2
CARRY = 0.8
SUBLANES = 8
LOAD_FLOPS = 2_000_000_000
SIDES_FLOPS = 3_000_000_000
FAR_FLOPS = 3_000_000_000
MIB = 1024 * 1024


def split_rows(count):
    inner = 1 << ((count.bit_length() - 1) // 2)
    return count // inner, inner


def swap_rows(value, shift):
    count = lax.axis_size("row")
    return lax.ppermute(value, "row", [(i, i ^ shift) for i in range(count)])


def swap_cores(value):
    return lax.ppermute(value, "col", [(0, 1), (1, 0)])


def call(kernel, out_shape, *operands, smem=0, flops=0):
    spaces = [pltpu.SMEM] * smem + [pltpu.VMEM] * (len(operands) - smem)
    size = sum(x.size * x.dtype.itemsize for x in (*operands, *jax.tree.leaves(out_shape)))
    return pl.pallas_call(
        kernel,
        out_shape=out_shape,
        in_specs=[pl.BlockSpec(memory_space=space) for space in spaces],
        out_specs=jax.tree.map(lambda _: pl.BlockSpec(memory_space=pltpu.VMEM), out_shape),
        compiler_params=pltpu.CompilerParams(vmem_limit_bytes=2 * size + 4 * MIB),
        cost_estimate=pl.CostEstimate(flops=flops, bytes_accessed=size, transcendentals=0),
    )(*operands)


def far_first(count):
    half = count // 2
    return [k for k in range(half, count)] + [k for k in range(1, half)]


def prepare_kernel(z_count, y_count, live, tile, *outs):
    strips, halves = outs[:z_count], outs[z_count:]
    row, col = lax.axis_index("row"), lax.axis_index("col")
    z, y = lax.div(row, y_count), lax.rem(row, y_count)
    width = tile.shape[1]
    out_row = lax.broadcasted_iota(jnp.int32, (2 * width, 2 * width), 0)
    in_row = lax.broadcasted_iota(jnp.int32, (2 * width, 2 * width), 1)
    side = lax.bitwise_xor((out_row >= width).astype(jnp.int32), col)
    spot = 2 * lax.rem(out_row, width) + side
    sort = jnp.where(in_row == spot, 1.0, 0.0).astype(jnp.bfloat16)
    for k in range(z_count):
        for j in range(y_count):
            block = lax.bitwise_xor(z, k) * y_count + lax.bitwise_xor(y, j)
            rows = tile[pl.ds(pl.multiple_of(block * 2 * width, 2 * width), 2 * width), :]
            sides = jnp.dot(sort, rows, preferred_element_type=jnp.float32)
            for i in range(2):
                keep = live[lax.bitwise_xor(col, i), 0, block] == 1
                piece = sides[i * width : (i + 1) * width]
                piece = jnp.where(keep, piece, jnp.zeros_like(piece)).astype(jnp.bfloat16)
                strips[k][i, j] = piece
                if j > 0:
                    halves[j - 1][i, k] = piece


def fold_kernel(y_count, first, *refs):
    keeps, taken, (total, *sends) = refs[:y_count], refs[y_count], refs[y_count + 1 :]
    total[...] = keeps[0][...] + taken[0]
    for j, send in enumerate(sends, 1):
        both = keeps[j][...] + taken[j]
        width = both.shape[0] - (SUBLANES if first else 0)
        send[:width, :] = both[:width].astype(jnp.bfloat16)
        if first:
            sums = jnp.concatenate([both[width:]] * 2, axis=0)
            high = sums.astype(jnp.bfloat16).astype(jnp.float32)
            middle = (sums - high).astype(jnp.bfloat16).astype(jnp.float32)
            row = lax.broadcasted_iota(jnp.int32, sums.shape, 0)
            terms = jnp.where(row == 0, high, jnp.where(row == 1, middle, sums - high - middle))
            send[width:, :] = terms.astype(jnp.bfloat16)


def join_kernel(*refs):
    parts, out = refs[:-1], refs[-1]
    start = 0
    for part in parts:
        out[start : start + part.shape[0]] = part[...]
        start += part.shape[0]


def join(parts, flops=0):
    rows = sum(x.shape[0] for x in parts)
    return call(join_kernel, jax.ShapeDtypeStruct((rows,) + parts[0].shape[1:], parts[0].dtype), *parts, flops=flops)


def load_kernel(*refs):
    strip, pieces, out = refs[0], refs[1:-1], refs[-1]
    sides, blocks, width, _ = strip.shape
    for i in range(sides):
        for j in range(blocks):
            out[i * blocks + j] = strip[i, j]
    spot = sides * blocks
    for piece in pieces:
        for top in range(0, piece.shape[0], width):
            for left in range(0, piece.shape[1], width):
                out[spot] = piece[top : top + width, left : left + width]
                spot += 1


def unload_kernel(y_count, *refs):
    pieces, loaded, out = refs[:-2], refs[-2], refs[-1]
    width, classes = loaded.shape[1], out.shape[1]
    start = 0
    for piece in pieces:
        out[start : start + piece.shape[0]] = piece[...]
        start += piece.shape[0]
    for spot in range(2 * y_count, loaded.shape[0], classes // width):
        for part in range(classes // width):
            out[start : start + width, part * width : (part + 1) * width] = loaded[spot + part]
        start += width


def block_of(strip, i, j, y_count):
    return strip[i * y_count + j] if len(strip.shape) == 3 else strip[i, j]


def far_kernel(*refs):
    strips, out = refs[:-1], refs[-1]
    for k, strip in enumerate(strips):
        out[k] = strip[1]


def other_kernel(far, own, loaded, out):
    z_count, y_count = out.shape[:2]
    for j in range(y_count):
        out[0, j] = own[1, j]
        out[1, j] = loaded[y_count + j]
    for spot, k in enumerate(k for k in far_first(z_count) if k > 1):
        out[k] = far[spot]


def seed_kernel(seed_class, seed_mask, base):
    width, classes = base.shape
    kind = jnp.where(seed_mask[...] == 1, seed_class[...], -1)
    kind = jnp.transpose(jnp.broadcast_to(kind, (width, width)))
    for start in range(0, classes, width):
        slots = lax.broadcasted_iota(jnp.int32, (width, width), 1) + start
        base[:, start : start + width] = jnp.where(kind == slots, 1.0 - CARRY, 0.0)


def spread_kernel(order, y_count, first, *refs):
    z_count = len(order)
    sent, refs = refs[:z_count], refs[z_count:]
    strips = dict(zip([0] + far_first(z_count), sent[:1] + refs))
    refs = refs[z_count - 1 :]
    halves, refs = refs[: y_count - 1], refs[y_count - 1 :]
    other, refs = refs[0], refs[1:]
    pieces, keeps, give = refs[: -y_count - 1], refs[-y_count - 1 : -1], refs[-1]
    if first:
        pieces, theirs = pieces[: len(pieces) // 2], pieces[len(pieces) // 2 :]
        theirs = jnp.concatenate([piece[...] for piece in theirs], axis=0)
    values = jnp.concatenate([piece[...] for piece in pieces], axis=0)
    depth, classes = values.shape
    width = depth // z_count
    ones = jnp.ones((SUBLANES, depth), jnp.bfloat16)

    def product(left, right, contract):
        return lax.dot_general(left, right, ((contract[:1], contract[1:]), ((), ())), preferred_element_type=jnp.float32)

    for i in (1, 0):
        for j in range(y_count):
            back = jnp.concatenate([sent[k][i, 0] if j == 0 else halves[j - 1][i, k] for k in order], axis=0)
            total = product(back, values, (0, 0))
            ahead = []
            if first and i == 0:
                ahead = [(0, values), (1, theirs)]
                ahead = [(jnp.concatenate([block_of(strips[k], s, j, y_count) for k in order], axis=1), v) for s, v in ahead]
            elif not first:
                ahead = [block_of(strips[k], 0, j, y_count) if i == 0 else other[k, j] for k in order]
                ahead = [(jnp.concatenate(ahead, axis=1), values)]
            for blocks, right in ahead:
                total += product(blocks, right, (1, 0))
            out = keeps[j] if i == 0 else give.at[j]
            out[:width, :] = total
            if first:
                sums = product(ones, back, (1, 0))
                for blocks, _ in ahead:
                    sums += product(ones, blocks, (1, 1))
                out[width:, :] = jnp.concatenate([sums] * (classes // width), axis=1)


def on_device(affinity, block_live, labels, seed_class, seed_mask):
    stripe, sides, width = affinity.shape
    count = lax.axis_size("row")
    z_count, y_count = split_rows(count)
    classes = labels.shape[1]

    strip = jax.ShapeDtypeStruct((2, y_count, width, width), jnp.bfloat16)
    half = jax.ShapeDtypeStruct((2, z_count, width, width), jnp.bfloat16)
    sent = call(
        lambda *refs: prepare_kernel(z_count, y_count, *refs),
        [strip] * z_count + [half] * (y_count - 1),
        block_live.transpose(1, 2, 0),
        affinity.reshape(stripe * sides, width),
        smem=1,
    )
    sent, halves = sent[:z_count], sent[z_count:]
    halves = [swap_rows(x, j + 1) for j, x in enumerate(halves)]
    have, order, bit = [labels], [0], z_count // 2
    while bit > 1:
        whole = have[0] if len(have) == 1 else join(have)
        have = [whole, swap_rows(whole, bit * y_count)]
        order = order + [k ^ bit for k in order]
        bit //= 2
    arrived = {k: swap_rows(sent[k], k * y_count) for k in far_first(z_count) if k > 1}
    blocks = 2 * y_count + len(order) * classes // width
    loaded = jax.ShapeDtypeStruct((blocks, width, width), jnp.bfloat16)
    arrived[1] = swap_rows(call(load_kernel, loaded, sent[1], *have, flops=LOAD_FLOPS), y_count)
    order = order + [k ^ 1 for k in order]
    values = jax.ShapeDtypeStruct((z_count * width, classes), jnp.bfloat16)
    values = call(lambda *refs: unload_kernel(y_count, *refs), values, *have, arrived[1])
    strips = [arrived[k] for k in far_first(z_count)]
    swapped = swap_cores(values)
    far_strips = [arrived[k] for k in far_first(z_count) if k > 1]
    far = jax.ShapeDtypeStruct((len(far_strips), y_count, width, width), jnp.bfloat16)
    far = call(far_kernel, far, *far_strips, flops=FAR_FLOPS)
    far = join([far], flops=SIDES_FLOPS)
    other = jax.ShapeDtypeStruct((z_count, y_count, width, width), jnp.bfloat16)
    other = swap_cores(call(other_kernel, other, far, sent[0], arrived[1]))
    pieces = [far, values, swapped]
    base = call(
        seed_kernel,
        jax.ShapeDtypeStruct((width, classes), jnp.float32),
        seed_class.reshape(1, width),
        seed_mask.reshape(1, width),
    )

    current, degree = labels, None
    for step in range(ITERS):
        if step > 0:
            order = [0] + far_first(z_count)
            pieces = [other, current] + [swap_rows(current, k * y_count) for k in order[1:]]
        height = width + (SUBLANES if step == 0 else 0)
        part = jax.ShapeDtypeStruct((height, classes), jnp.float32)
        parts = jax.ShapeDtypeStruct((y_count, height, classes), jnp.float32)
        *keeps, give = call(
            lambda *refs: spread_kernel(order, y_count, step == 0, *refs),
            [part] * y_count + [parts],
            *sent,
            *strips,
            *halves,
            *pieces,
            flops=2 * 2 * 2 * y_count * z_count * width * width * classes,
        )
        taken = swap_cores(give)
        send = jax.ShapeDtypeStruct((width + (2 * SUBLANES if step == 0 else 0), classes), jnp.bfloat16)
        total, *sends = call(
            lambda *refs: fold_kernel(y_count, step == 0, *refs), [part] + [send] * (y_count - 1), *keeps, taken
        )
        sends = [swap_rows(x, j + 1).astype(jnp.float32) for j, x in enumerate(sends)]
        spread = sum((x[:width] for x in sends), total[:width])
        if step == 0:
            sums = sum((x[width : width + 3, :width].sum(axis=0) for x in sends), total[width, :width])
            degree = 1.0 + 0.5 * sums[:, None]
        mixed = CARRY * (0.5 * spread + current.astype(jnp.float32)) / degree
        current = (mixed + base).astype(jnp.bfloat16)
    return current


def solution(mesh):
    return jax.shard_map(
        on_device,
        mesh=mesh,
        in_specs=(
            P(("groups", "col"), None, "row"),
            P(("groups", "col"), None, "row"),
            P(("groups", "col", "row"), None),
            P(("groups", "col", "row")),
            P(("groups", "col", "row")),
        ),
        out_specs=P(("groups", "col", "row"), None),
        check_vma=False,
    )
```

```python
import jax
import jax.numpy as jnp
from jax import lax
from jax.experimental import pallas as pl
from jax.experimental.pallas import tpu as pltpu
from jax.sharding import PartitionSpec as P

ITERS = 2
CARRY = 0.8
SUBLANES = 8
LEAD_FLOPS = 2_000_000_000
LOAD_FLOPS = 2_000_000_000
SIDES_FLOPS = 3_000_000_000
FAR_FLOPS = 3_000_000_000
MIB = 1024 * 1024


def split_rows(count):
    inner = 1 << ((count.bit_length() - 1) // 2)
    return count // inner, inner


def swap_rows(value, shift):
    count = lax.axis_size("row")
    return lax.ppermute(value, "row", [(i, i ^ shift) for i in range(count)])


def swap_cores(value):
    return lax.ppermute(value, "col", [(0, 1), (1, 0)])


def call(kernel, out_shape, *operands, smem=0, flops=0):
    spaces = [pltpu.SMEM] * smem + [pltpu.VMEM] * (len(operands) - smem)
    size = sum(x.size * x.dtype.itemsize for x in (*operands, *jax.tree.leaves(out_shape)))
    return pl.pallas_call(
        kernel,
        out_shape=out_shape,
        in_specs=[pl.BlockSpec(memory_space=space) for space in spaces],
        out_specs=jax.tree.map(lambda _: pl.BlockSpec(memory_space=pltpu.VMEM), out_shape),
        compiler_params=pltpu.CompilerParams(vmem_limit_bytes=2 * size + 4 * MIB),
        cost_estimate=pl.CostEstimate(flops=flops, bytes_accessed=size, transcendentals=0),
    )(*operands)


def far_first(count):
    half = count // 2
    return [k for k in range(half, count)] + [k for k in range(1, half)]


def prepare_kernel(z_count, y_count, live, tile, lead, *outs):
    strips = outs
    row, col = lax.axis_index("row"), lax.axis_index("col")
    z, y = lax.div(row, y_count), lax.rem(row, y_count)
    width = tile.shape[1]
    out_row = lax.broadcasted_iota(jnp.int32, (2 * width, 2 * width), 0)
    in_row = lax.broadcasted_iota(jnp.int32, (2 * width, 2 * width), 1)
    side = lax.bitwise_xor((out_row >= width).astype(jnp.int32), col)
    spot = 2 * lax.rem(out_row, width) + side
    sort = jnp.where(in_row == spot, 1.0, 0.0).astype(jnp.bfloat16)
    for k in range(z_count):
        for j in range(y_count):
            block = lax.bitwise_xor(z, k) * y_count + lax.bitwise_xor(y, j)
            rows = tile[pl.ds(pl.multiple_of(block * 2 * width, 2 * width), 2 * width), :]
            sides = jnp.dot(sort, rows, preferred_element_type=jnp.float32)
            for i in range(2):
                keep = live[lax.bitwise_xor(col, i), 0, block] == 1
                piece = sides[i * width : (i + 1) * width]
                piece = jnp.where(keep, piece, jnp.zeros_like(piece)).astype(jnp.bfloat16)
                strips[k][i, j] = piece


def fold_kernel(y_count, first, *refs):
    keeps, taken, (total, *sends) = refs[:y_count], refs[y_count], refs[y_count + 1 :]
    total[...] = keeps[0][...] + taken[0]
    for j, send in enumerate(sends, 1):
        both = keeps[j][...] + taken[j]
        width = both.shape[0] - (SUBLANES if first else 0)
        send[:width, :] = both[:width].astype(jnp.bfloat16)
        if first:
            sums = jnp.concatenate([both[width:]] * 2, axis=0)
            high = sums.astype(jnp.bfloat16).astype(jnp.float32)
            middle = (sums - high).astype(jnp.bfloat16).astype(jnp.float32)
            row = lax.broadcasted_iota(jnp.int32, sums.shape, 0)
            terms = jnp.where(row == 0, high, jnp.where(row == 1, middle, sums - high - middle))
            send[width:, :] = terms.astype(jnp.bfloat16)


def join_kernel(*refs):
    parts, out = refs[:-1], refs[-1]
    start = 0
    for part in parts:
        out[start : start + part.shape[0]] = part[...]
        start += part.shape[0]


def join(parts, flops=0):
    rows = sum(x.shape[0] for x in parts)
    return call(join_kernel, jax.ShapeDtypeStruct((rows,) + parts[0].shape[1:], parts[0].dtype), *parts, flops=flops)


def load_kernel(z_count, y_count, *refs):
    strips, refs = refs[:z_count], refs[z_count:]
    halves, refs = refs[1 - y_count :], refs[: 1 - y_count]
    strip, pieces, out = strips[1], refs[:-1], refs[-1]
    sides, blocks, width, _ = strip.shape
    for j, half in enumerate(halves, 1):
        for k in range(z_count):
            for i in range(sides):
                half[i, k] = strips[k][i, j]
    for i in range(sides):
        for j in range(blocks):
            out[i * blocks + j] = strip[i, j]
    spot = sides * blocks
    for piece in pieces:
        for top in range(0, piece.shape[0], width):
            for left in range(0, piece.shape[1], width):
                out[spot] = piece[top : top + width, left : left + width]
                spot += 1


def unload_kernel(y_count, *refs):
    pieces, loaded, out = refs[:-2], refs[-2], refs[-1]
    width, classes = loaded.shape[1], out.shape[1]
    start = 0
    for piece in pieces:
        out[start : start + piece.shape[0]] = piece[...]
        start += piece.shape[0]
    for spot in range(2 * y_count, loaded.shape[0], classes // width):
        for part in range(classes // width):
            out[start : start + width, part * width : (part + 1) * width] = loaded[spot + part]
        start += width


def block_of(strip, i, j, y_count):
    return strip[i * y_count + j] if len(strip.shape) == 3 else strip[i, j]


def far_kernel(*refs):
    strips, out = refs[:-1], refs[-1]
    for k, strip in enumerate(strips):
        out[k] = strip[1]


def other_kernel(far, own, loaded, out):
    z_count, y_count = out.shape[:2]
    for j in range(y_count):
        out[0, j] = own[1, j]
        out[1, j] = loaded[y_count + j]
    for spot, k in enumerate(k for k in far_first(z_count) if k > 1):
        out[k] = far[spot]


def lead_kernel(out):
    out[...] = jnp.zeros_like(out)


def seed_kernel(seed_class, seed_mask, base):
    width, classes = base.shape
    kind = jnp.where(seed_mask[...] == 1, seed_class[...], -1)
    kind = jnp.transpose(jnp.broadcast_to(kind, (width, width)))
    for start in range(0, classes, width):
        slots = lax.broadcasted_iota(jnp.int32, (width, width), 1) + start
        base[:, start : start + width] = jnp.where(kind == slots, 1.0 - CARRY, 0.0)


def spread_kernel(order, y_count, first, *refs):
    z_count = len(order)
    sent, refs = refs[:z_count], refs[z_count:]
    strips = dict(zip([0] + far_first(z_count), sent[:1] + refs))
    refs = refs[z_count - 1 :]
    halves, refs = refs[: y_count - 1], refs[y_count - 1 :]
    other, refs = refs[0], refs[1:]
    pieces, keeps, give = refs[: -y_count - 1], refs[-y_count - 1 : -1], refs[-1]
    if first:
        pieces, theirs = pieces[: len(pieces) // 2], pieces[len(pieces) // 2 :]
        theirs = jnp.concatenate([piece[...] for piece in theirs], axis=0)
    values = jnp.concatenate([piece[...] for piece in pieces], axis=0)
    depth, classes = values.shape
    width = depth // z_count
    ones = jnp.ones((SUBLANES, depth), jnp.bfloat16)

    def product(left, right, contract):
        return lax.dot_general(left, right, ((contract[:1], contract[1:]), ((), ())), preferred_element_type=jnp.float32)

    for i in (1, 0):
        for j in range(y_count):
            back = jnp.concatenate([sent[k][i, 0] if j == 0 else halves[j - 1][i, k] for k in order], axis=0)
            total = product(back, values, (0, 0))
            ahead = []
            if first and i == 0:
                ahead = [(0, values), (1, theirs)]
                ahead = [(jnp.concatenate([block_of(strips[k], s, j, y_count) for k in order], axis=1), v) for s, v in ahead]
            elif not first:
                ahead = [block_of(strips[k], 0, j, y_count) if i == 0 else other[k, j] for k in order]
                ahead = [(jnp.concatenate(ahead, axis=1), values)]
            for blocks, right in ahead:
                total += product(blocks, right, (1, 0))
            out = keeps[j] if i == 0 else give.at[j]
            out[:width, :] = total
            if first:
                sums = product(ones, back, (1, 0))
                for blocks, _ in ahead:
                    sums += product(ones, blocks, (1, 1))
                out[width:, :] = jnp.concatenate([sums] * (classes // width), axis=1)


def on_device(affinity, block_live, labels, seed_class, seed_mask):
    stripe, sides, width = affinity.shape
    count = lax.axis_size("row")
    z_count, y_count = split_rows(count)
    classes = labels.shape[1]

    strip = jax.ShapeDtypeStruct((2, y_count, width, width), jnp.bfloat16)
    half = jax.ShapeDtypeStruct((2, z_count, width, width), jnp.bfloat16)
    sent = call(
        lambda *refs: prepare_kernel(z_count, y_count, *refs),
        [strip] * z_count,
        block_live.transpose(1, 2, 0),
        affinity.reshape(stripe * sides, width),
        call(lead_kernel, jax.ShapeDtypeStruct((SUBLANES, width), jnp.float32), flops=LEAD_FLOPS),
        smem=1,
    )
    have, order, bit = [labels], [0], z_count // 2
    while bit > 1:
        whole = have[0] if len(have) == 1 else join(have)
        have = [whole, swap_rows(whole, bit * y_count)]
        order = order + [k ^ bit for k in order]
        bit //= 2
    arrived = {k: swap_rows(sent[k], k * y_count) for k in far_first(z_count) if k > 1}
    blocks = 2 * y_count + len(order) * classes // width
    loaded = jax.ShapeDtypeStruct((blocks, width, width), jnp.bfloat16)
    loaded, *halves = call(
        lambda *refs: load_kernel(z_count, y_count, *refs),
        [loaded] + [half] * (y_count - 1),
        *sent,
        *have,
        flops=LOAD_FLOPS,
    )
    arrived[1] = swap_rows(loaded, y_count)
    halves = [swap_rows(x, j + 1) for j, x in enumerate(halves)]
    order = order + [k ^ 1 for k in order]
    values = jax.ShapeDtypeStruct((z_count * width, classes), jnp.bfloat16)
    values = call(lambda *refs: unload_kernel(y_count, *refs), values, *have, arrived[1])
    strips = [arrived[k] for k in far_first(z_count)]
    swapped = swap_cores(values)
    far_strips = [arrived[k] for k in far_first(z_count) if k > 1]
    far = jax.ShapeDtypeStruct((len(far_strips), y_count, width, width), jnp.bfloat16)
    far = call(far_kernel, far, *far_strips, flops=FAR_FLOPS)
    far = join([far], flops=SIDES_FLOPS)
    other = jax.ShapeDtypeStruct((z_count, y_count, width, width), jnp.bfloat16)
    other = swap_cores(call(other_kernel, other, far, sent[0], arrived[1]))
    pieces = [far, values, swapped]
    base = call(
        seed_kernel,
        jax.ShapeDtypeStruct((width, classes), jnp.float32),
        seed_class.reshape(1, width),
        seed_mask.reshape(1, width),
    )

    current, degree = labels, None
    for step in range(ITERS):
        if step > 0:
            order = [0] + far_first(z_count)
            pieces = [other, current] + [swap_rows(current, k * y_count) for k in order[1:]]
        height = width + (SUBLANES if step == 0 else 0)
        part = jax.ShapeDtypeStruct((height, classes), jnp.float32)
        parts = jax.ShapeDtypeStruct((y_count, height, classes), jnp.float32)
        *keeps, give = call(
            lambda *refs: spread_kernel(order, y_count, step == 0, *refs),
            [part] * y_count + [parts],
            *sent,
            *strips,
            *halves,
            *pieces,
            flops=2 * 2 * 2 * y_count * z_count * width * width * classes,
        )
        taken = swap_cores(give)
        send = jax.ShapeDtypeStruct((width + (2 * SUBLANES if step == 0 else 0), classes), jnp.bfloat16)
        total, *sends = call(
            lambda *refs: fold_kernel(y_count, step == 0, *refs), [part] + [send] * (y_count - 1), *keeps, taken
        )
        sends = [swap_rows(x, j + 1).astype(jnp.float32) for j, x in enumerate(sends)]
        spread = sum((x[:width] for x in sends), total[:width])
        if step == 0:
            sums = sum((x[width : width + 3, :width].sum(axis=0) for x in sends), total[width, :width])
            degree = 1.0 + 0.5 * sums[:, None]
        mixed = CARRY * (0.5 * spread + current.astype(jnp.float32)) / degree
        current = (mixed + base).astype(jnp.bfloat16)
    return current


def solution(mesh):
    return jax.shard_map(
        on_device,
        mesh=mesh,
        in_specs=(
            P(("groups", "col"), None, "row"),
            P(("groups", "col"), None, "row"),
            P(("groups", "col", "row"), None),
            P(("groups", "col", "row")),
            P(("groups", "col", "row")),
        ),
        out_specs=P(("groups", "col", "row"), None),
        check_vma=False,
    )
```

```python
import jax
import jax.numpy as jnp
from jax import lax
from jax.experimental import pallas as pl
from jax.experimental.pallas import tpu as pltpu
from jax.sharding import PartitionSpec as P

ITERS = 2
CARRY = 0.8
SUBLANES = 8
LEAD_FLOPS = 2_000_000_000
HALVES_FLOPS = 4_000_000_000
MIB = 1024 * 1024


def split_rows(count):
    high = 1 << ((count.bit_length() - 1) // 2)
    return count // high, high


def swap_rows(value, shift):
    count = lax.axis_size("row")
    return lax.ppermute(value, "row", [(i, i ^ shift) for i in range(count)])


def swap_cores(value):
    return lax.ppermute(value, "col", [(0, 1), (1, 0)])


def call(kernel, out_shape, *operands, smem=0, flops=0):
    spaces = [pltpu.SMEM] * smem + [pltpu.VMEM] * (len(operands) - smem)
    size = sum(x.size * x.dtype.itemsize for x in (*operands, *jax.tree.leaves(out_shape)))
    return pl.pallas_call(
        kernel,
        out_shape=out_shape,
        in_specs=[pl.BlockSpec(memory_space=space) for space in spaces],
        out_specs=jax.tree.map(lambda _: pl.BlockSpec(memory_space=pltpu.VMEM), out_shape),
        compiler_params=pltpu.CompilerParams(vmem_limit_bytes=2 * size + 4 * MIB),
        cost_estimate=pl.CostEstimate(flops=flops, bytes_accessed=size, transcendentals=0),
    )(*operands)


def far_first(count):
    half = count // 2
    return [k for k in range(half, count)] + [k for k in range(1, half)]


def prepare_kernel(low_count, high_count, live, tile, labels, lead, own, *outs):
    strips, halves = outs[: low_count - 1], outs[low_count - 1 :]
    row, col = lax.axis_index("row"), lax.axis_index("col")
    high, low = lax.div(row, low_count), lax.rem(row, low_count)
    width = tile.shape[1]
    out_row = lax.broadcasted_iota(jnp.int32, (2 * width, 2 * width), 0)
    in_row = lax.broadcasted_iota(jnp.int32, (2 * width, 2 * width), 1)
    side = lax.bitwise_xor((out_row >= width).astype(jnp.int32), col)
    spot = 2 * lax.rem(out_row, width) + side
    sort = jnp.where(in_row == spot, 1.0, 0.0).astype(jnp.bfloat16)
    for j in reversed(range(high_count)):
        for k in range(low_count):
            block = lax.bitwise_xor(high, j) * low_count + lax.bitwise_xor(low, k)
            rows = tile[pl.ds(pl.multiple_of(block * 2 * width, 2 * width), 2 * width), :]
            sides = jnp.dot(sort, rows, preferred_element_type=jnp.float32)
            for i in range(2):
                keep = live[lax.bitwise_xor(col, i), 0, block] == 1
                piece = sides[i * width : (i + 1) * width]
                piece = jnp.where(keep, piece, jnp.zeros_like(piece)).astype(jnp.bfloat16)
                out = own if k == 0 else strips[k - 1]
                out[i * high_count + j] = piece
                if j > 0:
                    halves[j - 1][i, k] = piece
    for strip in strips:
        for part in range(labels.shape[1] // width):
            strip[2 * high_count + part] = labels[:, part * width : (part + 1) * width]


def fold_kernel(high_count, first, *refs):
    keeps, taken, (total, *sends) = refs[:high_count], refs[high_count], refs[high_count + 1 :]
    total[...] = keeps[0][...] + taken[0]
    for j, send in enumerate(sends, 1):
        both = keeps[j][...] + taken[j]
        width = both.shape[0] - (SUBLANES if first else 0)
        send[:width, :] = both[:width].astype(jnp.bfloat16)
        if first:
            sums = jnp.concatenate([both[width:]] * 2, axis=0)
            high = sums.astype(jnp.bfloat16).astype(jnp.float32)
            middle = (sums - high).astype(jnp.bfloat16).astype(jnp.float32)
            row = lax.broadcasted_iota(jnp.int32, sums.shape, 0)
            terms = jnp.where(row == 0, high, jnp.where(row == 1, middle, sums - high - middle))
            send[width:, :] = terms.astype(jnp.bfloat16)


def unload_kernel(spot, own, *refs):
    strips, out = refs[:-1], refs[-1]
    width, classes = own.shape
    out[:width] = own[...]
    for k, strip in enumerate(strips, 1):
        for part in range(classes // width):
            out[k * width : (k + 1) * width, part * width : (part + 1) * width] = strip[spot + part]


def guard_kernel(*refs):
    refs[-1][...] = jnp.zeros_like(refs[-1])


def other_kernel(*refs):
    strips, out = refs[:-1], refs[-1]
    high_count = out.shape[1]
    for k, strip in enumerate(strips):
        for j in range(high_count):
            out[k, j] = strip[high_count + j]


def lead_kernel(out):
    out[...] = jnp.zeros_like(out)


def seed_kernel(seed_class, seed_mask, base):
    width, classes = base.shape
    kind = jnp.where(seed_mask[...] == 1, seed_class[...], -1)
    kind = jnp.transpose(jnp.broadcast_to(kind, (width, width)))
    for start in range(0, classes, width):
        slots = lax.broadcasted_iota(jnp.int32, (width, width), 1) + start
        base[:, start : start + width] = jnp.where(kind == slots, 1.0 - CARRY, 0.0)


def spread_kernel(low_count, high_count, first, *refs):
    sent, refs = refs[:low_count], refs[low_count:]
    strips, refs = sent[:1] + refs[: low_count - 1], refs[low_count - 1 :]
    halves, refs = refs[: high_count - 1], refs[high_count - 1 :]
    other, refs = refs[0], refs[1:]
    pieces, keeps, give = refs[: -high_count - 1], refs[-high_count - 1 : -1], refs[-1]
    if first:
        pieces, theirs = pieces[:1], pieces[1][...]
    values = jnp.concatenate([piece[...] for piece in pieces], axis=0)
    depth, classes = values.shape
    width = depth // low_count
    ones = jnp.ones((SUBLANES, depth), jnp.bfloat16)

    def product(left, right, contract):
        return lax.dot_general(left, right, ((contract[:1], contract[1:]), ((), ())), preferred_element_type=jnp.float32)

    def strip_blocks(i, j):
        return jnp.concatenate([strip[i * high_count + j] for strip in strips], axis=1)

    for i in (1, 0):
        for j in range(high_count):
            back = [sent[k][i * high_count] if j == 0 else halves[j - 1][i, k] for k in range(low_count)]
            back = jnp.concatenate(back, axis=0)
            total = product(back, values, (0, 0))
            ahead = []
            if first and i == 0:
                ahead = [(strip_blocks(0, j), values), (strip_blocks(1, j), theirs)]
            elif not first and i == 0:
                ahead = [(strip_blocks(0, j), values)]
            elif not first:
                ahead = [(jnp.concatenate([other[k, j] for k in range(low_count)], axis=1), values)]
            for blocks, right in ahead:
                total += product(blocks, right, (1, 0))
            out = keeps[j] if i == 0 else give.at[j]
            out[:width, :] = total
            if first:
                sums = product(ones, back, (1, 0))
                for blocks, _ in ahead:
                    sums += product(ones, blocks, (1, 1))
                out[width:, :] = jnp.concatenate([sums] * (classes // width), axis=1)


def on_device(affinity, block_live, labels, seed_class, seed_mask):
    stripe, sides, width = affinity.shape
    count = lax.axis_size("row")
    low_count, high_count = split_rows(count)
    classes = labels.shape[1]

    blocks = 2 * high_count
    own = jax.ShapeDtypeStruct((blocks, width, width), jnp.bfloat16)
    strip = jax.ShapeDtypeStruct((blocks + classes // width, width, width), jnp.bfloat16)
    half = jax.ShapeDtypeStruct((2, low_count, width, width), jnp.bfloat16)
    sent = call(
        lambda *refs: prepare_kernel(low_count, high_count, *refs),
        [own] + [strip] * (low_count - 1) + [half] * (high_count - 1),
        block_live.transpose(1, 2, 0),
        affinity.reshape(stripe * sides, width),
        labels,
        call(lead_kernel, jax.ShapeDtypeStruct((SUBLANES, width), jnp.float32), flops=LEAD_FLOPS),
        smem=1,
    )
    sent, halves = sent[:low_count], sent[low_count:]
    halves = [swap_rows(x, (j + 1) * low_count) for j, x in enumerate(halves)]
    arrived = {k: swap_rows(sent[k], k) for k in far_first(low_count)}
    strips = [arrived[k] for k in range(1, low_count)]
    values = jax.ShapeDtypeStruct((low_count * width, classes), jnp.bfloat16)
    values = call(lambda *refs: unload_kernel(blocks, *refs), values, labels, *strips)
    swapped = swap_cores(values)
    mark = jax.ShapeDtypeStruct((SUBLANES, width), jnp.float32)
    mark = call(guard_kernel, mark, *halves, flops=HALVES_FLOPS)
    other = jax.ShapeDtypeStruct((low_count, high_count, width, width), jnp.bfloat16)
    other = swap_cores(call(other_kernel, other, sent[0], *strips))
    pieces = [mark, values, swapped]
    base = call(
        seed_kernel,
        jax.ShapeDtypeStruct((width, classes), jnp.float32),
        seed_class.reshape(1, width),
        seed_mask.reshape(1, width),
    )

    current, degree = labels, None
    for step in range(ITERS):
        if step > 0:
            taken = {k: swap_rows(current, k) for k in far_first(low_count)}
            pieces = [other, current] + [taken[k] for k in range(1, low_count)]
        height = width + (SUBLANES if step == 0 else 0)
        part = jax.ShapeDtypeStruct((height, classes), jnp.float32)
        parts = jax.ShapeDtypeStruct((high_count, height, classes), jnp.float32)
        *keeps, give = call(
            lambda *refs: spread_kernel(low_count, high_count, step == 0, *refs),
            [part] * high_count + [parts],
            *sent,
            *strips,
            *halves,
            *pieces,
            flops=2 * 2 * 2 * high_count * low_count * width * width * classes,
        )
        taken = swap_cores(give)
        send = jax.ShapeDtypeStruct((width + (2 * SUBLANES if step == 0 else 0), classes), jnp.bfloat16)
        total, *sends = call(
            lambda *refs: fold_kernel(high_count, step == 0, *refs), [part] + [send] * (high_count - 1), *keeps, taken
        )
        sends = [swap_rows(x, (j + 1) * low_count).astype(jnp.float32) for j, x in enumerate(sends)]
        spread = sum((x[:width] for x in sends), total[:width])
        if step == 0:
            sums = sum((x[width : width + 3, :width].sum(axis=0) for x in sends), total[width, :width])
            degree = 1.0 + 0.5 * sums[:, None]
        mixed = CARRY * (0.5 * spread + current.astype(jnp.float32)) / degree
        current = (mixed + base).astype(jnp.bfloat16)
    return current


def solution(mesh):
    return jax.shard_map(
        on_device,
        mesh=mesh,
        in_specs=(
            P(("groups", "col"), None, "row"),
            P(("groups", "col"), None, "row"),
            P(("groups", "col", "row"), None),
            P(("groups", "col", "row")),
            P(("groups", "col", "row")),
        ),
        out_specs=P(("groups", "col", "row"), None),
        check_vma=False,
    )
```

```python
import jax
import jax.numpy as jnp
from jax import lax
from jax.experimental import pallas as pl
from jax.experimental.pallas import tpu as pltpu
from jax.sharding import PartitionSpec as P

ITERS = 2
CARRY = 0.8
SUBLANES = 8
LANES = 128
LEAD_FLOPS = 2_000_000_000
PAIR_FLOPS = 4_000_000_000
STRIPS_FLOPS = 3_000_000_000
MARK_FLOPS = 3_000_000_000
MIB = 1024 * 1024


def split_rows(count):
    inner = 1 << ((count.bit_length() - 1) // 2)
    return count // inner, inner


def swap_rows(value, shift):
    count = lax.axis_size("row")
    return lax.ppermute(value, "row", [(i, i ^ shift) for i in range(count)])


def swap_cores(value):
    return lax.ppermute(value, "col", [(0, 1), (1, 0)])


def call(kernel, out_shape, *operands, smem=0, flops=0):
    spaces = [pltpu.SMEM] * smem + [pltpu.VMEM] * (len(operands) - smem)
    size = sum(x.size * x.dtype.itemsize for x in (*operands, *jax.tree.leaves(out_shape)))
    return pl.pallas_call(
        kernel,
        out_shape=out_shape,
        in_specs=[pl.BlockSpec(memory_space=space) for space in spaces],
        out_specs=jax.tree.map(lambda _: pl.BlockSpec(memory_space=pltpu.VMEM), out_shape),
        compiler_params=pltpu.CompilerParams(vmem_limit_bytes=2 * size + 4 * MIB),
        cost_estimate=pl.CostEstimate(flops=flops, bytes_accessed=size, transcendentals=0),
    )(*operands)


def far_first(count):
    half = count // 2
    return [k for k in range(half, count)] + [k for k in range(1, half)]


def prepare_kernel(z_count, y_count, live, tile, lead, *outs):
    strips, other = outs[:z_count], outs[z_count]
    row, col = lax.axis_index("row"), lax.axis_index("col")
    z, y = lax.div(row, y_count), lax.rem(row, y_count)
    width = tile.shape[1]
    out_row = lax.broadcasted_iota(jnp.int32, (2 * width, 2 * width), 0)
    in_row = lax.broadcasted_iota(jnp.int32, (2 * width, 2 * width), 1)
    side = lax.bitwise_xor((out_row >= width).astype(jnp.int32), col)
    spot = 2 * lax.rem(out_row, width) + side
    sort = jnp.where(in_row == spot, 1.0, 0.0).astype(jnp.bfloat16)
    for k in range(z_count):
        for j in range(y_count):
            block = lax.bitwise_xor(z, k) * y_count + lax.bitwise_xor(y, j)
            rows = tile[pl.ds(pl.multiple_of(block * 2 * width, 2 * width), 2 * width), :]
            sides = jnp.dot(sort, rows, preferred_element_type=jnp.float32)
            for i in range(2):
                keep = live[lax.bitwise_xor(col, i), 0, block] == 1
                piece = sides[i * width : (i + 1) * width]
                piece = jnp.where(keep, piece, jnp.zeros_like(piece)).astype(jnp.bfloat16)
                strips[k][i, j] = piece
                if i == 1:
                    other[k, j] = piece


def halves_kernel(z_count, *refs):
    strips, from_core, halves = refs[:z_count], refs[z_count], refs[z_count + 1 :]
    for j, half in enumerate(halves, 1):
        for k in range(z_count):
            half[0, k] = strips[k][0, j]
            half[1, k] = from_core[k, j]


def join_kernel(*refs):
    parts, out = refs[:-1], refs[-1]
    start = 0
    for part in parts:
        out[start : start + part.shape[0]] = part[...]
        start += part.shape[0]


def join(parts, flops=0):
    rows = sum(x.shape[0] for x in parts)
    return call(join_kernel, jax.ShapeDtypeStruct((rows,) + parts[0].shape[1:], parts[0].dtype), *parts, flops=flops)


def guard_kernel(*refs):
    refs[-1][...] = jnp.zeros_like(refs[-1])


def guard(parts, flops):
    return call(guard_kernel, jax.ShapeDtypeStruct((SUBLANES, LANES), jnp.float32), *parts, flops=flops)


def lead_kernel(out):
    out[...] = jnp.zeros_like(out)


def seed_kernel(seed_class, seed_mask, base):
    width, classes = base.shape
    kind = jnp.where(seed_mask[...] == 1, seed_class[...], -1)
    kind = jnp.transpose(jnp.broadcast_to(kind, (width, width)))
    for start in range(0, classes, width):
        slots = lax.broadcasted_iota(jnp.int32, (width, width), 1) + start
        base[:, start : start + width] = jnp.where(kind == slots, 1.0 - CARRY, 0.0)


def spread_kernel(order, y_count, first, *refs):
    z_count = len(order)
    sent, refs = refs[:z_count], refs[z_count:]
    strips = dict(zip([0] + far_first(z_count), sent[:1] + refs))
    refs = refs[z_count - 1 :]
    from_core, halves, refs = refs[0], refs[1:y_count], refs[y_count:]
    (ours, theirs), outs = refs[:2], refs[-y_count:]
    values = jnp.concatenate([ours[...], theirs[...]], axis=0)
    depth, classes = values.shape
    width = depth // (2 * z_count)
    ones = jnp.ones((SUBLANES, depth), jnp.bfloat16)

    def product(left, right, contract):
        return lax.dot_general(left, right, ((contract[:1], contract[1:]), ((), ())), preferred_element_type=jnp.float32)

    def back_block(i, j, k):
        if j > 0:
            return halves[j - 1][i, k]
        return sent[k][0, 0] if i == 0 else from_core[k, 0]

    for j, out in reversed(list(enumerate(outs))):
        back = jnp.concatenate([back_block(i, j, k) for i in range(2) for k in order], axis=0)
        ahead = jnp.concatenate([strips[k][i, j] for i in range(2) for k in order], axis=1)
        total = product(back, values, (0, 0)) + product(ahead, values, (1, 0))
        out[:width, :] = total.astype(out.dtype)
        if first:
            sums = product(ones, back, (1, 0)) + product(ones, ahead, (1, 1))
            sums = jnp.concatenate([sums] * (classes // width), axis=1)
            if j > 0:
                sums = jnp.concatenate([sums] * 2, axis=0)
                high = sums.astype(jnp.bfloat16).astype(jnp.float32)
                middle = (sums - high).astype(jnp.bfloat16).astype(jnp.float32)
                row = lax.broadcasted_iota(jnp.int32, sums.shape, 0)
                sums = jnp.where(row == 0, high, jnp.where(row == 1, middle, sums - high - middle))
            out[width:, :] = sums.astype(out.dtype)


def on_device(affinity, block_live, labels, seed_class, seed_mask):
    stripe, sides, width = affinity.shape
    count = lax.axis_size("row")
    z_count, y_count = split_rows(count)
    classes = labels.shape[1]

    strip = jax.ShapeDtypeStruct((2, y_count, width, width), jnp.bfloat16)
    half = jax.ShapeDtypeStruct((2, z_count, width, width), jnp.bfloat16)
    *sent, other = call(
        lambda *refs: prepare_kernel(z_count, y_count, *refs),
        [strip] * z_count + [jax.ShapeDtypeStruct((z_count, y_count, width, width), jnp.bfloat16)],
        block_live.transpose(1, 2, 0),
        affinity.reshape(stripe * sides, width),
        call(lead_kernel, jax.ShapeDtypeStruct((SUBLANES, width), jnp.float32), flops=LEAD_FLOPS),
        smem=1,
    )
    from_core = swap_cores(other)
    halves = call(lambda *refs: halves_kernel(z_count, *refs), [half] * (y_count - 1), *sent, from_core)
    halves = [swap_rows(x, j + 1) for j, x in enumerate(halves)]
    arrived = {k: swap_rows(sent[k], k * y_count) for k in far_first(z_count)}
    strips = [arrived[k] for k in far_first(z_count)]
    mark = guard([guard(strips, STRIPS_FLOPS)] + halves, MARK_FLOPS)
    have, order, bit = [labels], [0], z_count // 2
    while bit:
        whole = have[0] if len(have) == 1 else join(have, PAIR_FLOPS)
        have = [whole, swap_rows(whole, bit * y_count)]
        order = order + [k ^ bit for k in order]
        bit //= 2
    base = call(
        seed_kernel,
        jax.ShapeDtypeStruct((width, classes), jnp.float32),
        seed_class.reshape(1, width),
        seed_mask.reshape(1, width),
    )

    current, degree = labels, None
    for step in range(ITERS):
        if step > 0:
            order = [0] + far_first(z_count)
            have = [current] + [swap_rows(current, k * y_count) for k in order[1:]]
        values = join(have)
        pieces = [values, swap_cores(values)] + ([mark] if step == 0 else [])
        extra = SUBLANES if step == 0 else 0
        total, *sends = call(
            lambda *refs: spread_kernel(order, y_count, step == 0, *refs),
            [jax.ShapeDtypeStruct((width + extra, classes), jnp.float32)]
            + [jax.ShapeDtypeStruct((width + 2 * extra, classes), jnp.bfloat16)] * (y_count - 1),
            *sent,
            *strips,
            from_core,
            *halves,
            *pieces,
            flops=2 * 2 * 2 * y_count * z_count * width * width * classes,
        )
        sends = [swap_rows(x, j + 1).astype(jnp.float32) for j, x in enumerate(sends)]
        spread = sum((x[:width] for x in sends), total[:width])
        if step == 0:
            sums = sum((x[width : width + 3, :width].sum(axis=0) for x in sends), total[width, :width])
            degree = 1.0 + 0.5 * sums[:, None]
        mixed = CARRY * (0.5 * spread + current.astype(jnp.float32)) / degree
        current = (mixed + base).astype(jnp.bfloat16)
    return current


def solution(mesh):
    return jax.shard_map(
        on_device,
        mesh=mesh,
        in_specs=(
            P(("groups", "col"), None, "row"),
            P(("groups", "col"), None, "row"),
            P(("groups", "col", "row"), None),
            P(("groups", "col", "row")),
            P(("groups", "col", "row")),
        ),
        out_specs=P(("groups", "col", "row"), None),
        check_vma=False,
    )
```

```python
import jax
import jax.numpy as jnp
from jax import lax
from jax.experimental import pallas as pl
from jax.experimental.pallas import tpu as pltpu
from jax.sharding import PartitionSpec as P

ITERS = 2
CARRY = 0.8
SUBLANES = 8
LANES = 128
LEAD_FLOPS = 2_000_000_000
PAIR_FLOPS = 4_000_000_000
STRIPS_FLOPS = 3_000_000_000
OURS_FLOPS = 3_000_000_000
MIB = 1024 * 1024


def split_rows(count):
    inner = 1 << ((count.bit_length() - 1) // 2)
    return count // inner, inner


def swap_rows(value, shift):
    count = lax.axis_size("row")
    return lax.ppermute(value, "row", [(i, i ^ shift) for i in range(count)])


def swap_cores(value):
    return lax.ppermute(value, "col", [(0, 1), (1, 0)])


def call(kernel, out_shape, *operands, smem=0, flops=0):
    spaces = [pltpu.SMEM] * smem + [pltpu.VMEM] * (len(operands) - smem)
    size = sum(x.size * x.dtype.itemsize for x in (*operands, *jax.tree.leaves(out_shape)))
    return pl.pallas_call(
        kernel,
        out_shape=out_shape,
        in_specs=[pl.BlockSpec(memory_space=space) for space in spaces],
        out_specs=jax.tree.map(lambda _: pl.BlockSpec(memory_space=pltpu.VMEM), out_shape),
        compiler_params=pltpu.CompilerParams(vmem_limit_bytes=2 * size + 4 * MIB),
        cost_estimate=pl.CostEstimate(flops=flops, bytes_accessed=size, transcendentals=0),
    )(*operands)


def far_first(count):
    half = count // 2
    return [half] + [k for k in range(1, count) if k != half]


def prepare_kernel(z_count, y_count, live, tile, lead, *outs):
    strips, other = outs[:z_count], outs[z_count]
    row, col = lax.axis_index("row"), lax.axis_index("col")
    z, y = lax.div(row, y_count), lax.rem(row, y_count)
    width = tile.shape[1]
    out_row = lax.broadcasted_iota(jnp.int32, (2 * width, 2 * width), 0)
    in_row = lax.broadcasted_iota(jnp.int32, (2 * width, 2 * width), 1)
    side = lax.bitwise_xor((out_row >= width).astype(jnp.int32), col)
    spot = 2 * lax.rem(out_row, width) + side
    sort = jnp.where(in_row == spot, 1.0, 0.0).astype(jnp.bfloat16)
    for k in range(z_count):
        for j in range(y_count):
            block = lax.bitwise_xor(z, k) * y_count + lax.bitwise_xor(y, j)
            rows = tile[pl.ds(pl.multiple_of(block * 2 * width, 2 * width), 2 * width), :]
            sides = jnp.dot(sort, rows, preferred_element_type=jnp.float32)
            for i in range(2):
                keep = live[lax.bitwise_xor(col, i), 0, block] == 1
                piece = sides[i * width : (i + 1) * width]
                piece = jnp.where(keep, piece, jnp.zeros_like(piece)).astype(jnp.bfloat16)
                strips[k][i, j] = piece
                if i == 1:
                    other[k, j] = piece


def halves_kernel(z_count, *refs):
    strips, from_core, halves = refs[:z_count], refs[z_count], refs[z_count + 1 :]
    for j, half in enumerate(halves, 1):
        for k in range(z_count):
            half[0, k] = strips[k][0, j]
            half[1, k] = from_core[k, j]


def join_kernel(*refs):
    parts, out = refs[:-1], refs[-1]
    start = 0
    for part in parts:
        out[start : start + part.shape[0]] = part[...]
        start += part.shape[0]


def join(parts, flops=0):
    rows = sum(x.shape[0] for x in parts)
    return call(join_kernel, jax.ShapeDtypeStruct((rows,) + parts[0].shape[1:], parts[0].dtype), *parts, flops=flops)


def guard_kernel(*refs):
    refs[-1][...] = jnp.zeros_like(refs[-1])


def guard(parts, flops):
    return call(guard_kernel, jax.ShapeDtypeStruct((SUBLANES, LANES), jnp.float32), *parts, flops=flops)


def lead_kernel(out):
    out[...] = jnp.zeros_like(out)


def seed_kernel(seed_class, seed_mask, base):
    width, classes = base.shape
    kind = jnp.where(seed_mask[...] == 1, seed_class[...], -1)
    kind = jnp.transpose(jnp.broadcast_to(kind, (width, width)))
    for start in range(0, classes, width):
        slots = lax.broadcasted_iota(jnp.int32, (width, width), 1) + start
        base[:, start : start + width] = jnp.where(kind == slots, 1.0 - CARRY, 0.0)


def product(left, right, contract):
    return lax.dot_general(left, right, ((contract[:1], contract[1:]), ((), ())), preferred_element_type=jnp.float32)


def blocks_of(order, y_count, refs, i, j):
    z_count = len(order)
    sent, refs = refs[:z_count], refs[z_count:]
    strips = dict(zip([0] + far_first(z_count), sent[:1] + refs))
    from_core, halves = refs[z_count - 1], refs[z_count:]

    def back_block(k):
        if j > 0:
            return halves[j - 1][i, k]
        return sent[k][0, 0] if i == 0 else from_core[k, 0]

    back = jnp.concatenate([back_block(k) for k in order], axis=0)
    return back, jnp.concatenate([strips[k][i, j] for k in order], axis=1)


def ours_kernel(order, y_count, first, *refs):
    blocks, values, outs = refs[: 2 * len(order) + y_count - 1], refs[2 * len(order) + y_count - 1], refs[-y_count:]
    values = values[...]
    depth, classes = values.shape
    width = depth // len(order)
    ones = jnp.ones((SUBLANES, depth), jnp.bfloat16)
    for j, out in enumerate(outs):
        back, ahead = blocks_of(order, y_count, blocks, 0, j)
        out[:width, :] = product(back, values, (0, 0)) + product(ahead, values, (1, 0))
        if first:
            sums = product(ones, back, (1, 0)) + product(ones, ahead, (1, 1))
            back, ahead = blocks_of(order, y_count, blocks, 1, j)
            sums += product(ones, back, (1, 0)) + product(ones, ahead, (1, 1))
            out[width:, :] = jnp.concatenate([sums] * (classes // width), axis=1)


def theirs_kernel(order, y_count, first, *refs):
    blocks, values, refs = refs[: 2 * len(order) + y_count - 1], refs[2 * len(order) + y_count - 1], refs[-2 * y_count :]
    values = values[...]
    width = values.shape[0] // len(order)
    for j in reversed(range(y_count)):
        part, out = refs[j], refs[y_count + j]
        back, ahead = blocks_of(order, y_count, blocks, 1, j)
        total = part[:width, :] + product(back, values, (0, 0)) + product(ahead, values, (1, 0))
        out[:width, :] = total.astype(out.dtype)
        if first:
            sums = part[width:, :]
            if j > 0:
                sums = jnp.concatenate([sums] * 2, axis=0)
                high = sums.astype(jnp.bfloat16).astype(jnp.float32)
                middle = (sums - high).astype(jnp.bfloat16).astype(jnp.float32)
                row = lax.broadcasted_iota(jnp.int32, sums.shape, 0)
                sums = jnp.where(row == 0, high, jnp.where(row == 1, middle, sums - high - middle))
            out[width:, :] = sums.astype(out.dtype)


def on_device(affinity, block_live, labels, seed_class, seed_mask):
    stripe, sides, width = affinity.shape
    count = lax.axis_size("row")
    z_count, y_count = split_rows(count)
    classes = labels.shape[1]

    strip = jax.ShapeDtypeStruct((2, y_count, width, width), jnp.bfloat16)
    half = jax.ShapeDtypeStruct((2, z_count, width, width), jnp.bfloat16)
    *sent, other = call(
        lambda *refs: prepare_kernel(z_count, y_count, *refs),
        [strip] * z_count + [jax.ShapeDtypeStruct((z_count, y_count, width, width), jnp.bfloat16)],
        block_live.transpose(1, 2, 0),
        affinity.reshape(stripe * sides, width),
        call(lead_kernel, jax.ShapeDtypeStruct((SUBLANES, width), jnp.float32), flops=LEAD_FLOPS),
        smem=1,
    )
    from_core = swap_cores(other)
    halves = call(lambda *refs: halves_kernel(z_count, *refs), [half] * (y_count - 1), *sent, from_core)
    halves = [swap_rows(x, j + 1) for j, x in enumerate(halves)]
    arrived = {k: swap_rows(sent[k], k * y_count) for k in far_first(z_count)}
    strips = [arrived[k] for k in far_first(z_count)]
    strips = [arrived[k] for k in far_first(z_count)]
    mark = guard(strips, STRIPS_FLOPS)
    blocks = [*sent, *strips, from_core, *halves]
    have, order, bit = [labels], [0], z_count // 2
    while bit:
        whole = have[0] if len(have) == 1 else join(have, PAIR_FLOPS)
        have = [whole, swap_rows(whole, bit * y_count)]
        order = order + [k ^ bit for k in order]
        bit //= 2
    base = call(
        seed_kernel,
        jax.ShapeDtypeStruct((width, classes), jnp.float32),
        seed_class.reshape(1, width),
        seed_mask.reshape(1, width),
    )

    current, degree = labels, None
    for step in range(ITERS):
        if step > 0:
            order = [0] + far_first(z_count)
            have = [current] + [swap_rows(current, k * y_count) for k in order[1:]]
        values = join(have)
        first = step == 0
        extra = SUBLANES if first else 0
        part = jax.ShapeDtypeStruct((width + extra, classes), jnp.float32)
        send = jax.ShapeDtypeStruct((width + 2 * extra, classes), jnp.bfloat16)
        parts = call(
            lambda *refs: ours_kernel(order, y_count, first, *refs),
            [part] * y_count,
            *blocks,
            values,
            *([mark] if first else []),
            flops=OURS_FLOPS if first else 0,
        )
        total, *sends = call(
            lambda *refs: theirs_kernel(order, y_count, first, *refs),
            [part] + [send] * (y_count - 1),
            *blocks,
            swap_cores(values),
            *parts,
        )
        sends = [swap_rows(x, j + 1).astype(jnp.float32) for j, x in enumerate(sends)]
        spread = sum((x[:width] for x in sends), total[:width])
        if first:
            sums = sum((x[width : width + 3, :width].sum(axis=0) for x in sends), total[width, :width])
            degree = 1.0 + 0.5 * sums[:, None]
        mixed = CARRY * (0.5 * spread + current.astype(jnp.float32)) / degree
        current = (mixed + base).astype(jnp.bfloat16)
    return current


def solution(mesh):
    return jax.shard_map(
        on_device,
        mesh=mesh,
        in_specs=(
            P(("groups", "col"), None, "row"),
            P(("groups", "col"), None, "row"),
            P(("groups", "col", "row"), None),
            P(("groups", "col", "row")),
            P(("groups", "col", "row")),
        ),
        out_specs=P(("groups", "col", "row"), None),
        check_vma=False,
    )
```

```python
import jax
import jax.numpy as jnp
from jax import lax
from jax.experimental import pallas as pl
from jax.experimental.pallas import tpu as pltpu
from jax.sharding import PartitionSpec as P

ITERS = 2
CARRY = 0.8
SUBLANES = 8
LANES = 128
LEAD_FLOPS = 2_000_000_000
PAIR_FLOPS = 4_000_000_000
STRIPS_FLOPS = 3_000_000_000
OURS_FLOPS = 3_000_000_000
MIB = 1024 * 1024


def split_rows(count):
    inner = 1 << ((count.bit_length() - 1) // 2)
    return count // inner, inner


def swap_rows(value, shift):
    count = lax.axis_size("row")
    return lax.ppermute(value, "row", [(i, i ^ shift) for i in range(count)])


def swap_cores(value):
    return lax.ppermute(value, "col", [(0, 1), (1, 0)])


def call(kernel, out_shape, *operands, smem=0, flops=0):
    spaces = [pltpu.SMEM] * smem + [pltpu.VMEM] * (len(operands) - smem)
    size = sum(x.size * x.dtype.itemsize for x in (*operands, *jax.tree.leaves(out_shape)))
    return pl.pallas_call(
        kernel,
        out_shape=out_shape,
        in_specs=[pl.BlockSpec(memory_space=space) for space in spaces],
        out_specs=jax.tree.map(lambda _: pl.BlockSpec(memory_space=pltpu.VMEM), out_shape),
        compiler_params=pltpu.CompilerParams(vmem_limit_bytes=2 * size + 4 * MIB),
        cost_estimate=pl.CostEstimate(flops=flops, bytes_accessed=size, transcendentals=0),
    )(*operands)


def far_first(count):
    half = count // 2
    return [half] + [k for k in range(1, count) if k != half]


def prepare_kernel(z_count, y_count, live, tile, lead, *outs):
    strips, other = outs[:z_count], outs[z_count]
    row, col = lax.axis_index("row"), lax.axis_index("col")
    z, y = lax.div(row, y_count), lax.rem(row, y_count)
    width = tile.shape[1]
    out_row = lax.broadcasted_iota(jnp.int32, (2 * width, 2 * width), 0)
    in_row = lax.broadcasted_iota(jnp.int32, (2 * width, 2 * width), 1)
    side = lax.bitwise_xor((out_row >= width).astype(jnp.int32), col)
    spot = 2 * lax.rem(out_row, width) + side
    sort = jnp.where(in_row == spot, 1.0, 0.0).astype(jnp.bfloat16)
    for k in range(z_count):
        for j in range(y_count):
            block = lax.bitwise_xor(z, k) * y_count + lax.bitwise_xor(y, j)
            rows = tile[pl.ds(pl.multiple_of(block * 2 * width, 2 * width), 2 * width), :]
            sides = jnp.dot(sort, rows, preferred_element_type=jnp.float32)
            for i in range(2):
                keep = live[lax.bitwise_xor(col, i), 0, block] == 1
                piece = sides[i * width : (i + 1) * width]
                piece = jnp.where(keep, piece, jnp.zeros_like(piece)).astype(jnp.bfloat16)
                strips[k][i, j] = piece
                if i == 1:
                    other[k, j] = piece


def halves_kernel(z_count, *refs):
    strips, from_core, halves = refs[:z_count], refs[z_count], refs[z_count + 1 :]
    for j, half in enumerate(halves, 1):
        for k in range(z_count):
            half[0, k] = strips[k][0, j]
            half[1, k] = from_core[k, j]


def join_kernel(*refs):
    parts, out = refs[:-1], refs[-1]
    start = 0
    for part in parts:
        out[start : start + part.shape[0]] = part[...]
        start += part.shape[0]


def join(parts, flops=0):
    rows = sum(x.shape[0] for x in parts)
    return call(join_kernel, jax.ShapeDtypeStruct((rows,) + parts[0].shape[1:], parts[0].dtype), *parts, flops=flops)


def guard_kernel(*refs):
    refs[-1][...] = jnp.zeros_like(refs[-1])


def guard(parts, flops):
    return call(guard_kernel, jax.ShapeDtypeStruct((SUBLANES, LANES), jnp.float32), *parts, flops=flops)


def lead_kernel(out):
    out[...] = jnp.zeros_like(out)


def seed_kernel(seed_class, seed_mask, base):
    width, classes = base.shape
    kind = jnp.where(seed_mask[...] == 1, seed_class[...], -1)
    kind = jnp.transpose(jnp.broadcast_to(kind, (width, width)))
    for start in range(0, classes, width):
        slots = lax.broadcasted_iota(jnp.int32, (width, width), 1) + start
        base[:, start : start + width] = jnp.where(kind == slots, 1.0 - CARRY, 0.0)


def product(left, right, contract):
    return lax.dot_general(left, right, ((contract[:1], contract[1:]), ((), ())), preferred_element_type=jnp.float32)


def blocks_of(order, y_count, refs, i, j):
    z_count = len(order)
    sent, refs = refs[:z_count], refs[z_count:]
    strips = dict(zip([0] + far_first(z_count), sent[:1] + refs))
    from_core, halves = refs[z_count - 1], refs[z_count:]

    def back_block(k):
        if j > 0:
            return halves[j - 1][i, k]
        return sent[k][0, 0] if i == 0 else from_core[k, 0]

    back = jnp.concatenate([back_block(k) for k in order], axis=0)
    return back, jnp.concatenate([strips[k][i, j] for k in order], axis=1)


def ours_kernel(order, y_count, first, *refs):
    blocks, values, outs = refs[: 2 * len(order) + y_count - 1], refs[2 * len(order) + y_count - 1], refs[-y_count:]
    values = values[...]
    depth, classes = values.shape
    width = depth // len(order)
    ones = jnp.ones((SUBLANES, depth), jnp.bfloat16)
    for j, out in enumerate(outs):
        back, ahead = blocks_of(order, y_count, blocks, 0, j)
        out[:width, :] = product(back, values, (0, 0)) + product(ahead, values, (1, 0))
        if first:
            sums = product(ones, back, (1, 0)) + product(ones, ahead, (1, 1))
            back, ahead = blocks_of(order, y_count, blocks, 1, j)
            sums += product(ones, back, (1, 0)) + product(ones, ahead, (1, 1))
            out[width:, :] = jnp.concatenate([sums] * (classes // width), axis=1)


def theirs_kernel(order, y_count, first, *refs):
    blocks, values, refs = refs[: 2 * len(order) + y_count - 1], refs[2 * len(order) + y_count - 1], refs[-2 * y_count :]
    values = values[...]
    width = values.shape[0] // len(order)
    for j in reversed(range(y_count)):
        part, out = refs[j], refs[y_count + j]
        back, ahead = blocks_of(order, y_count, blocks, 1, j)
        total = part[:width, :] + product(back, values, (0, 0)) + product(ahead, values, (1, 0))
        out[:width, :] = total.astype(out.dtype)
        if first:
            sums = part[width:, :]
            if j > 0:
                sums = jnp.concatenate([sums] * 2, axis=0)
                high = sums.astype(jnp.bfloat16).astype(jnp.float32)
                middle = (sums - high).astype(jnp.bfloat16).astype(jnp.float32)
                row = lax.broadcasted_iota(jnp.int32, sums.shape, 0)
                sums = jnp.where(row == 0, high, jnp.where(row == 1, middle, sums - high - middle))
            out[width:, :] = sums.astype(out.dtype)


def on_device(affinity, block_live, labels, seed_class, seed_mask):
    stripe, sides, width = affinity.shape
    count = lax.axis_size("row")
    z_count, y_count = split_rows(count)
    classes = labels.shape[1]

    strip = jax.ShapeDtypeStruct((2, y_count, width, width), jnp.bfloat16)
    half = jax.ShapeDtypeStruct((2, z_count, width, width), jnp.bfloat16)
    *sent, other = call(
        lambda *refs: prepare_kernel(z_count, y_count, *refs),
        [strip] * z_count + [jax.ShapeDtypeStruct((z_count, y_count, width, width), jnp.bfloat16)],
        block_live.transpose(1, 2, 0),
        affinity.reshape(stripe * sides, width),
        call(lead_kernel, jax.ShapeDtypeStruct((SUBLANES, width), jnp.float32), flops=LEAD_FLOPS),
        smem=1,
    )
    from_core = swap_cores(other)
    halves = call(lambda *refs: halves_kernel(z_count, *refs), [half] * (y_count - 1), *sent, from_core)
    halves = [swap_rows(x, j + 1) for j, x in enumerate(halves)]
    arrived = {k: swap_rows(sent[k], k * y_count) for k in far_first(z_count)}
    strips = [arrived[k] for k in far_first(z_count)]
    strips = [arrived[k] for k in far_first(z_count)]
    mark = guard(strips, STRIPS_FLOPS)
    blocks = [*sent, *strips, from_core, *halves]
    have, order, bit = [labels], [0], z_count // 2
    while bit:
        whole = have[0] if len(have) == 1 else join(have, PAIR_FLOPS)
        have = [whole, swap_rows(whole, bit * y_count)]
        order = order + [k ^ bit for k in order]
        bit //= 2
    base = call(
        seed_kernel,
        jax.ShapeDtypeStruct((width, classes), jnp.float32),
        seed_class.reshape(1, width),
        seed_mask.reshape(1, width),
    )

    current, degree = labels, None
    for step in range(ITERS):
        if step > 0:
            order = [0] + far_first(z_count)[::-1]
            have = [current] + [swap_rows(current, k * y_count) for k in order[1:]]
        values = join(have)
        first = step == 0
        extra = SUBLANES if first else 0
        part = jax.ShapeDtypeStruct((width + extra, classes), jnp.float32)
        send = jax.ShapeDtypeStruct((width + 2 * extra, classes), jnp.bfloat16)
        parts = call(
            lambda *refs: ours_kernel(order, y_count, first, *refs),
            [part] * y_count,
            *blocks,
            values,
            *([mark] if first else []),
            flops=OURS_FLOPS if first else 0,
        )
        total, *sends = call(
            lambda *refs: theirs_kernel(order, y_count, first, *refs),
            [part] + [send] * (y_count - 1),
            *blocks,
            swap_cores(values),
            *parts,
        )
        sends = [swap_rows(x, j + 1).astype(jnp.float32) for j, x in enumerate(sends)]
        spread = sum((x[:width] for x in sends), total[:width])
        if first:
            sums = sum((x[width : width + 3, :width].sum(axis=0) for x in sends), total[width, :width])
            degree = 1.0 + 0.5 * sums[:, None]
        mixed = CARRY * (0.5 * spread + current.astype(jnp.float32)) / degree
        current = (mixed + base).astype(jnp.bfloat16)
    return current


def solution(mesh):
    return jax.shard_map(
        on_device,
        mesh=mesh,
        in_specs=(
            P(("groups", "col"), None, "row"),
            P(("groups", "col"), None, "row"),
            P(("groups", "col", "row"), None),
            P(("groups", "col", "row")),
            P(("groups", "col", "row")),
        ),
        out_specs=P(("groups", "col", "row"), None),
        check_vma=False,
    )
```

```python
import jax
import jax.numpy as jnp
from jax import lax
from jax.experimental import pallas as pl
from jax.experimental.pallas import tpu as pltpu
from jax.sharding import PartitionSpec as P

ITERS = 2
CARRY = 0.8
SUBLANES = 8
LANES = 128
LEAD_FLOPS = 2_000_000_000
PAIR_FLOPS = 4_000_000_000
STRIPS_FLOPS = 3_000_000_000
OURS_FLOPS = 3_000_000_000
MIB = 1024 * 1024


def split_rows(count):
    inner = 1 << ((count.bit_length() - 1) // 2)
    return count // inner, inner


def swap_rows(value, shift):
    count = lax.axis_size("row")
    return lax.ppermute(value, "row", [(i, i ^ shift) for i in range(count)])


def swap_cores(value):
    return lax.ppermute(value, "col", [(0, 1), (1, 0)])


def call(kernel, out_shape, *operands, smem=0, flops=0):
    spaces = [pltpu.SMEM] * smem + [pltpu.VMEM] * (len(operands) - smem)
    size = sum(x.size * x.dtype.itemsize for x in (*operands, *jax.tree.leaves(out_shape)))
    return pl.pallas_call(
        kernel,
        out_shape=out_shape,
        in_specs=[pl.BlockSpec(memory_space=space) for space in spaces],
        out_specs=jax.tree.map(lambda _: pl.BlockSpec(memory_space=pltpu.VMEM), out_shape),
        compiler_params=pltpu.CompilerParams(vmem_limit_bytes=2 * size + 4 * MIB),
        cost_estimate=pl.CostEstimate(flops=flops, bytes_accessed=size, transcendentals=0),
    )(*operands)


def others(count):
    return list(range(1, count))


def others_late(count):
    half = count // 2
    return list(range(half + 1, count)) + list(range(1, half)) + [half]


def prepare_kernel(z_count, y_count, live, tile, lead, *outs):
    strips, other = outs[:z_count], outs[z_count]
    row, col = lax.axis_index("row"), lax.axis_index("col")
    z, y = lax.div(row, y_count), lax.rem(row, y_count)
    width = tile.shape[1]
    out_row = lax.broadcasted_iota(jnp.int32, (2 * width, 2 * width), 0)
    in_row = lax.broadcasted_iota(jnp.int32, (2 * width, 2 * width), 1)
    side = lax.bitwise_xor((out_row >= width).astype(jnp.int32), col)
    spot = 2 * lax.rem(out_row, width) + side
    sort = jnp.where(in_row == spot, 1.0, 0.0).astype(jnp.bfloat16)
    for k in range(z_count):
        for j in range(y_count):
            block = lax.bitwise_xor(z, k) * y_count + lax.bitwise_xor(y, j)
            rows = tile[pl.ds(pl.multiple_of(block * 2 * width, 2 * width), 2 * width), :]
            sides = jnp.dot(sort, rows, preferred_element_type=jnp.float32)
            for i in range(2):
                keep = live[lax.bitwise_xor(col, i), 0, block] == 1
                piece = sides[i * width : (i + 1) * width]
                piece = jnp.where(keep, piece, jnp.zeros_like(piece)).astype(jnp.bfloat16)
                strips[k][i, j] = piece
                if i == 1:
                    other[k, j] = piece


def halves_kernel(z_count, *refs):
    strips, from_core, halves = refs[:z_count], refs[z_count], refs[z_count + 1 :]
    for j, half in enumerate(halves, 1):
        for k in range(z_count):
            half[0, k] = strips[k][0, j]
            half[1, k] = from_core[k, j]


def join_kernel(*refs):
    parts, out = refs[:-1], refs[-1]
    start = 0
    for part in parts:
        out[start : start + part.shape[0]] = part[...]
        start += part.shape[0]


def join(parts, flops=0):
    rows = sum(x.shape[0] for x in parts)
    return call(join_kernel, jax.ShapeDtypeStruct((rows,) + parts[0].shape[1:], parts[0].dtype), *parts, flops=flops)


def guard_kernel(*refs):
    refs[-1][...] = jnp.zeros_like(refs[-1])


def guard(parts, flops):
    return call(guard_kernel, jax.ShapeDtypeStruct((SUBLANES, LANES), jnp.float32), *parts, flops=flops)


def lead_kernel(out):
    out[...] = jnp.zeros_like(out)


def seed_kernel(seed_class, seed_mask, base):
    width, classes = base.shape
    kind = jnp.where(seed_mask[...] == 1, seed_class[...], -1)
    kind = jnp.transpose(jnp.broadcast_to(kind, (width, width)))
    for start in range(0, classes, width):
        slots = lax.broadcasted_iota(jnp.int32, (width, width), 1) + start
        base[:, start : start + width] = jnp.where(kind == slots, 1.0 - CARRY, 0.0)


def product(left, right, contract):
    return lax.dot_general(left, right, ((contract[:1], contract[1:]), ((), ())), preferred_element_type=jnp.float32)


def blocks_of(order, y_count, refs, i, j):
    z_count = len(order)
    sent, refs = refs[:z_count], refs[z_count:]
    strips = dict(zip([0] + others(z_count), sent[:1] + refs))
    from_core, halves = refs[z_count - 1], refs[z_count:]

    def back_block(k):
        if j > 0:
            return halves[j - 1][i, k]
        return sent[k][0, 0] if i == 0 else from_core[k, 0]

    back = jnp.concatenate([back_block(k) for k in order], axis=0)
    return back, jnp.concatenate([strips[k][i, j] for k in order], axis=1)


def ours_kernel(order, y_count, first, *refs):
    blocks, values, outs = refs[: 2 * len(order) + y_count - 1], refs[2 * len(order) + y_count - 1], refs[-y_count:]
    values = values[...]
    depth, classes = values.shape
    width = depth // len(order)
    ones = jnp.ones((SUBLANES, depth), jnp.bfloat16)
    for j, out in enumerate(outs):
        back, ahead = blocks_of(order, y_count, blocks, 0, j)
        out[:width, :] = product(back, values, (0, 0)) + product(ahead, values, (1, 0))
        if first:
            sums = product(ones, back, (1, 0)) + product(ones, ahead, (1, 1))
            back, ahead = blocks_of(order, y_count, blocks, 1, j)
            sums += product(ones, back, (1, 0)) + product(ones, ahead, (1, 1))
            out[width:, :] = jnp.concatenate([sums] * (classes // width), axis=1)


def theirs_kernel(order, y_count, first, *refs):
    blocks, values, refs = refs[: 2 * len(order) + y_count - 1], refs[2 * len(order) + y_count - 1], refs[-2 * y_count :]
    values = values[...]
    width = values.shape[0] // len(order)
    for j in reversed(range(y_count)):
        part, out = refs[j], refs[y_count + j]
        back, ahead = blocks_of(order, y_count, blocks, 1, j)
        total = part[:width, :] + product(back, values, (0, 0)) + product(ahead, values, (1, 0))
        out[:width, :] = total.astype(out.dtype)
        if first:
            sums = part[width:, :]
            if j > 0:
                sums = jnp.concatenate([sums] * 2, axis=0)
                high = sums.astype(jnp.bfloat16).astype(jnp.float32)
                middle = (sums - high).astype(jnp.bfloat16).astype(jnp.float32)
                row = lax.broadcasted_iota(jnp.int32, sums.shape, 0)
                sums = jnp.where(row == 0, high, jnp.where(row == 1, middle, sums - high - middle))
            out[width:, :] = sums.astype(out.dtype)


def on_device(affinity, block_live, labels, seed_class, seed_mask):
    stripe, sides, width = affinity.shape
    count = lax.axis_size("row")
    z_count, y_count = split_rows(count)
    classes = labels.shape[1]

    strip = jax.ShapeDtypeStruct((2, y_count, width, width), jnp.bfloat16)
    half = jax.ShapeDtypeStruct((2, z_count, width, width), jnp.bfloat16)
    *sent, other = call(
        lambda *refs: prepare_kernel(z_count, y_count, *refs),
        [strip] * z_count + [jax.ShapeDtypeStruct((z_count, y_count, width, width), jnp.bfloat16)],
        block_live.transpose(1, 2, 0),
        affinity.reshape(stripe * sides, width),
        call(lead_kernel, jax.ShapeDtypeStruct((SUBLANES, width), jnp.float32), flops=LEAD_FLOPS),
        smem=1,
    )
    from_core = swap_cores(other)
    halves = call(lambda *refs: halves_kernel(z_count, *refs), [half] * (y_count - 1), *sent, from_core)
    halves = [swap_rows(x, j + 1) for j, x in enumerate(halves)]
    arrived = {k: swap_rows(sent[k], k * y_count) for k in others(z_count)}
    strips = [arrived[k] for k in others(z_count)]
    strips = [arrived[k] for k in others(z_count)]
    mark = guard(strips, STRIPS_FLOPS)
    blocks = [*sent, *strips, from_core, *halves]
    have, order, bit = [labels], [0], z_count // 2
    while bit:
        whole = have[0] if len(have) == 1 else join(have, PAIR_FLOPS)
        have = [whole, swap_rows(whole, bit * y_count)]
        order = order + [k ^ bit for k in order]
        bit //= 2
    base = call(
        seed_kernel,
        jax.ShapeDtypeStruct((width, classes), jnp.float32),
        seed_class.reshape(1, width),
        seed_mask.reshape(1, width),
    )

    current, degree = labels, None
    for step in range(ITERS):
        if step > 0:
            order = [0] + others_late(z_count)
            have = [current] + [swap_rows(current, k * y_count) for k in order[1:]]
        values = join(have)
        first = step == 0
        extra = SUBLANES if first else 0
        part = jax.ShapeDtypeStruct((width + extra, classes), jnp.float32)
        send = jax.ShapeDtypeStruct((width + 2 * extra, classes), jnp.bfloat16)
        parts = call(
            lambda *refs: ours_kernel(order, y_count, first, *refs),
            [part] * y_count,
            *blocks,
            values,
            *([mark] if first else []),
            flops=OURS_FLOPS if first else 0,
        )
        total, *sends = call(
            lambda *refs: theirs_kernel(order, y_count, first, *refs),
            [part] + [send] * (y_count - 1),
            *blocks,
            swap_cores(values),
            *parts,
        )
        sends = [swap_rows(x, j + 1).astype(jnp.float32) for j, x in enumerate(sends)]
        spread = sum((x[:width] for x in sends), total[:width])
        if first:
            sums = sum((x[width : width + 3, :width].sum(axis=0) for x in sends), total[width, :width])
            degree = 1.0 + 0.5 * sums[:, None]
        mixed = CARRY * (0.5 * spread + current.astype(jnp.float32)) / degree
        current = (mixed + base).astype(jnp.bfloat16)
    return current


def solution(mesh):
    return jax.shard_map(
        on_device,
        mesh=mesh,
        in_specs=(
            P(("groups", "col"), None, "row"),
            P(("groups", "col"), None, "row"),
            P(("groups", "col", "row"), None),
            P(("groups", "col", "row")),
            P(("groups", "col", "row")),
        ),
        out_specs=P(("groups", "col", "row"), None),
        check_vma=False,
    )
```

```python
import jax
import jax.numpy as jnp
from jax import lax
from jax.experimental import pallas as pl
from jax.experimental.pallas import tpu as pltpu
from jax.sharding import PartitionSpec as P

ITERS = 2
CARRY = 0.8
SUBLANES = 8
LANES = 128
LEAD_FLOPS = 2_000_000_000
PAIR_FLOPS = 4_000_000_000
STRIPS_FLOPS = 3_000_000_000
OURS_FLOPS = 3_000_000_000
MIB = 1024 * 1024


def split_rows(count):
    inner = 1 << ((count.bit_length() - 1) // 2)
    return count // inner, inner


def swap_rows(value, shift):
    count = lax.axis_size("row")
    return lax.ppermute(value, "row", [(i, i ^ shift) for i in range(count)])


def swap_cores(value):
    return lax.ppermute(value, "col", [(0, 1), (1, 0)])


def call(kernel, out_shape, *operands, smem=0, flops=0):
    spaces = [pltpu.SMEM] * smem + [pltpu.VMEM] * (len(operands) - smem)
    size = sum(x.size * x.dtype.itemsize for x in (*operands, *jax.tree.leaves(out_shape)))
    return pl.pallas_call(
        kernel,
        out_shape=out_shape,
        in_specs=[pl.BlockSpec(memory_space=space) for space in spaces],
        out_specs=jax.tree.map(lambda _: pl.BlockSpec(memory_space=pltpu.VMEM), out_shape),
        compiler_params=pltpu.CompilerParams(vmem_limit_bytes=2 * size + 4 * MIB),
        cost_estimate=pl.CostEstimate(flops=flops, bytes_accessed=size, transcendentals=0),
    )(*operands)


def others(count):
    return list(range(1, count))


def others_late(count):
    half = count // 2
    return list(range(half + 1, count)) + list(range(1, half)) + [half]


def prepare_kernel(z_count, y_count, live, tile, lead, *outs):
    strips, other = outs[:z_count], outs[z_count]
    row, col = lax.axis_index("row"), lax.axis_index("col")
    z, y = lax.div(row, y_count), lax.rem(row, y_count)
    width = tile.shape[1]
    for k in range(z_count):
        for j in range(y_count):
            block = lax.bitwise_xor(z, k) * y_count + lax.bitwise_xor(y, j)
            rows = tile.at[pl.ds(pl.multiple_of(block * 2 * width, 2 * width), 2 * width)]
            pair = []
            for side in range(2):
                piece = rows[pl.ds(side, width, stride=2), :]
                pair.append(jnp.where(live[side, 0, block] == 1, piece, jnp.zeros_like(piece)))
                strips[k][lax.bitwise_xor(col, side), j] = pair[-1]
            other[k, j] = jnp.where(col == 0, pair[1], pair[0])


def halves_kernel(z_count, *refs):
    strips, from_core, halves = refs[:z_count], refs[z_count], refs[z_count + 1 :]
    for j, half in enumerate(halves, 1):
        for k in range(z_count):
            half[0, k] = strips[k][0, j]
            half[1, k] = from_core[k, j]


def join_kernel(*refs):
    parts, out = refs[:-1], refs[-1]
    start = 0
    for part in parts:
        out[start : start + part.shape[0]] = part[...]
        start += part.shape[0]


def join(parts, flops=0):
    rows = sum(x.shape[0] for x in parts)
    return call(join_kernel, jax.ShapeDtypeStruct((rows,) + parts[0].shape[1:], parts[0].dtype), *parts, flops=flops)


def guard_kernel(*refs):
    refs[-1][...] = jnp.zeros_like(refs[-1])


def guard(parts, flops):
    return call(guard_kernel, jax.ShapeDtypeStruct((SUBLANES, LANES), jnp.float32), *parts, flops=flops)


def lead_kernel(out):
    out[...] = jnp.zeros_like(out)


def seed_kernel(seed_class, seed_mask, base):
    width, classes = base.shape
    kind = jnp.where(seed_mask[...] == 1, seed_class[...], -1)
    kind = jnp.transpose(jnp.broadcast_to(kind, (width, width)))
    for start in range(0, classes, width):
        slots = lax.broadcasted_iota(jnp.int32, (width, width), 1) + start
        base[:, start : start + width] = jnp.where(kind == slots, 1.0 - CARRY, 0.0)


def product(left, right, contract):
    return lax.dot_general(left, right, ((contract[:1], contract[1:]), ((), ())), preferred_element_type=jnp.float32)


def blocks_of(order, y_count, refs, i, j):
    z_count = len(order)
    sent, refs = refs[:z_count], refs[z_count:]
    strips = dict(zip([0] + others(z_count), sent[:1] + refs))
    from_core, halves = refs[z_count - 1], refs[z_count:]

    def back_block(k):
        if j > 0:
            return halves[j - 1][i, k]
        return sent[k][0, 0] if i == 0 else from_core[k, 0]

    back = jnp.concatenate([back_block(k) for k in order], axis=0)
    return back, jnp.concatenate([strips[k][i, j] for k in order], axis=1)


def ours_kernel(order, y_count, first, *refs):
    count = 2 * len(order) + y_count - 1
    blocks, pieces, outs = refs[:count], refs[count:-y_count], refs[-y_count:]
    pieces = pieces[:-1] if first else pieces
    values = jnp.concatenate([piece[...] for piece in pieces], axis=0)
    depth, classes = values.shape
    width = depth // len(order)
    ones = jnp.ones((SUBLANES, depth), jnp.bfloat16)
    for j, out in enumerate(outs):
        back, ahead = blocks_of(order, y_count, blocks, 0, j)
        out[:width, :] = product(back, values, (0, 0)) + product(ahead, values, (1, 0))
        if first:
            sums = product(ones, back, (1, 0)) + product(ones, ahead, (1, 1))
            back, ahead = blocks_of(order, y_count, blocks, 1, j)
            sums += product(ones, back, (1, 0)) + product(ones, ahead, (1, 1))
            out[width:, :] = jnp.concatenate([sums] * (classes // width), axis=1)


def theirs_kernel(order, y_count, wanted, first, *refs):
    count = 2 * len(order) + y_count - 1
    blocks, pieces, refs = refs[:count], refs[count : -2 * len(wanted)], refs[-2 * len(wanted) :]
    values = jnp.concatenate([piece[...] for piece in pieces], axis=0)
    width = values.shape[0] // len(order)
    for j, part, out in zip(wanted, refs[: len(wanted)], refs[len(wanted) :]):
        back, ahead = blocks_of(order, y_count, blocks, 1, j)
        total = part[:width, :] + product(back, values, (0, 0)) + product(ahead, values, (1, 0))
        out[:width, :] = total.astype(out.dtype)
        if first:
            sums = part[width:, :]
            if j > 0:
                sums = jnp.concatenate([sums] * 2, axis=0)
                high = sums.astype(jnp.bfloat16).astype(jnp.float32)
                middle = (sums - high).astype(jnp.bfloat16).astype(jnp.float32)
                row = lax.broadcasted_iota(jnp.int32, sums.shape, 0)
                sums = jnp.where(row == 0, high, jnp.where(row == 1, middle, sums - high - middle))
            out[width:, :] = sums.astype(out.dtype)


def on_device(affinity, block_live, labels, seed_class, seed_mask):
    stripe, sides, width = affinity.shape
    count = lax.axis_size("row")
    z_count, y_count = split_rows(count)
    classes = labels.shape[1]

    strip = jax.ShapeDtypeStruct((2, y_count, width, width), jnp.bfloat16)
    half = jax.ShapeDtypeStruct((2, z_count, width, width), jnp.bfloat16)
    *sent, other = call(
        lambda *refs: prepare_kernel(z_count, y_count, *refs),
        [strip] * z_count + [jax.ShapeDtypeStruct((z_count, y_count, width, width), jnp.bfloat16)],
        block_live.transpose(1, 2, 0),
        affinity.reshape(stripe * sides, width),
        call(lead_kernel, jax.ShapeDtypeStruct((SUBLANES, width), jnp.float32), flops=LEAD_FLOPS),
        smem=1,
    )
    from_core = swap_cores(other)
    halves = call(lambda *refs: halves_kernel(z_count, *refs), [half] * (y_count - 1), *sent, from_core)
    halves = [swap_rows(x, j + 1) for j, x in enumerate(halves)]
    arrived = {k: swap_rows(sent[k], k * y_count) for k in others(z_count)}
    strips = [arrived[k] for k in others(z_count)]
    strips = [arrived[k] for k in others(z_count)]
    mark = guard(strips, STRIPS_FLOPS)
    blocks = [*sent, *strips, from_core, *halves]
    have, order, bit = [labels], [0], z_count // 2
    while bit:
        whole = have[0] if len(have) == 1 else join(have, PAIR_FLOPS)
        have = [whole, swap_rows(whole, bit * y_count)]
        order = order + [k ^ bit for k in order]
        bit //= 2
    base = call(
        seed_kernel,
        jax.ShapeDtypeStruct((width, classes), jnp.float32),
        seed_class.reshape(1, width),
        seed_mask.reshape(1, width),
    )

    current, degree = labels, None
    for step in range(ITERS):
        if step > 0:
            order = [0] + others_late(z_count)
            have = [current] + [swap_rows(current, k * y_count) for k in order[1:]]
        first = step == 0
        have = [join(have)]
        extra = SUBLANES if first else 0
        part = jax.ShapeDtypeStruct((width + extra, classes), jnp.float32)
        send = jax.ShapeDtypeStruct((width + 2 * extra, classes), jnp.bfloat16)
        parts = call(
            lambda *refs: ours_kernel(order, y_count, first, *refs),
            [part] * y_count,
            *blocks,
            *have,
            *([mark] if first else []),
            flops=OURS_FLOPS if first else 0,
        )
        have = [swap_cores(x) for x in have]
        wanted = range(1, y_count)
        sends = call(
            lambda *refs: theirs_kernel(order, y_count, wanted, first, *refs), [send] * (y_count - 1), *blocks, *have, *parts[1:]
        )
        (total,) = call(lambda *refs: theirs_kernel(order, y_count, [0], first, *refs), [part], *blocks, *have, parts[0])
        sends = [swap_rows(x, j + 1).astype(jnp.float32) for j, x in enumerate(sends)]
        spread = sum((x[:width] for x in sends), total[:width])
        if first:
            sums = sum((x[width : width + 3, :width].sum(axis=0) for x in sends), total[width, :width])
            degree = 1.0 + 0.5 * sums[:, None]
        mixed = CARRY * (0.5 * spread + current.astype(jnp.float32)) / degree
        current = (mixed + base).astype(jnp.bfloat16)
    return current


def solution(mesh):
    return jax.shard_map(
        on_device,
        mesh=mesh,
        in_specs=(
            P(("groups", "col"), None, "row"),
            P(("groups", "col"), None, "row"),
            P(("groups", "col", "row"), None),
            P(("groups", "col", "row")),
            P(("groups", "col", "row")),
        ),
        out_specs=P(("groups", "col", "row"), None),
        check_vma=False,
    )
```

```python
import jax
import jax.numpy as jnp
from jax import lax
from jax.experimental import pallas as pl
from jax.experimental.pallas import tpu as pltpu
from jax.sharding import PartitionSpec as P

ITERS = 2
CARRY = 0.8
SUBLANES = 8
LANES = 128
LEAD_FLOPS = 2_000_000_000
PAIR_FLOPS = 4_000_000_000
STRIPS_FLOPS = 3_000_000_000
OURS_FLOPS = 3_000_000_000
LAST_FLOPS = 2_000_000_000
MIB = 1024 * 1024


def split_rows(count):
    inner = 1 << ((count.bit_length() - 1) // 2)
    return count // inner, inner


def swap_rows(value, shift):
    count = lax.axis_size("row")
    return lax.ppermute(value, "row", [(i, i ^ shift) for i in range(count)])


def swap_cores(value):
    return lax.ppermute(value, "col", [(0, 1), (1, 0)])


def call(kernel, out_shape, *operands, smem=0, flops=0):
    spaces = [pltpu.SMEM] * smem + [pltpu.VMEM] * (len(operands) - smem)
    size = sum(x.size * x.dtype.itemsize for x in (*operands, *jax.tree.leaves(out_shape)))
    return pl.pallas_call(
        kernel,
        out_shape=out_shape,
        in_specs=[pl.BlockSpec(memory_space=space) for space in spaces],
        out_specs=jax.tree.map(lambda _: pl.BlockSpec(memory_space=pltpu.VMEM), out_shape),
        compiler_params=pltpu.CompilerParams(vmem_limit_bytes=2 * size + 4 * MIB),
        cost_estimate=pl.CostEstimate(flops=flops, bytes_accessed=size, transcendentals=0),
    )(*operands)


def others(count):
    return list(range(1, count))


def others_late(count):
    half = count // 2
    return list(range(1, half)) + list(range(half + 1, count)) + [half]


def prepare_kernel(z_count, y_count, live, tile, lead, *outs):
    strips = outs
    row, col = lax.axis_index("row"), lax.axis_index("col")
    z, y = lax.div(row, y_count), lax.rem(row, y_count)
    width = tile.shape[1]
    for k in range(z_count):
        for j in range(y_count):
            block = lax.bitwise_xor(z, k) * y_count + lax.bitwise_xor(y, j)
            rows = tile.at[pl.ds(pl.multiple_of(block * 2 * width, 2 * width), 2 * width)]
            for side in range(2):
                piece = rows[pl.ds(side, width, stride=2), :]
                keep = live[side, 0, block] == 1
                strips[k][lax.bitwise_xor(col, side), j] = jnp.where(keep, piece, jnp.zeros_like(piece))


def other_kernel(*refs):
    strips, out = refs[:-1], refs[-1]
    for k, strip in enumerate(strips):
        out[k] = strip[1]


def halves_kernel(z_count, *refs):
    strips, from_core, halves = refs[:z_count], refs[z_count], refs[z_count + 1 :]
    for j, half in enumerate(halves, 1):
        for k in range(z_count):
            half[0, k] = strips[k][0, j]
            half[1, k] = from_core[k, j]


def join_kernel(*refs):
    parts, out = refs[:-1], refs[-1]
    start = 0
    for part in parts:
        out[start : start + part.shape[0]] = part[...]
        start += part.shape[0]


def join(parts, flops=0):
    rows = sum(x.shape[0] for x in parts)
    return call(join_kernel, jax.ShapeDtypeStruct((rows,) + parts[0].shape[1:], parts[0].dtype), *parts, flops=flops)


def guard_kernel(*refs):
    refs[-1][...] = jnp.zeros_like(refs[-1])


def guard(parts, flops):
    return call(guard_kernel, jax.ShapeDtypeStruct((SUBLANES, LANES), jnp.float32), *parts, flops=flops)


def lead_kernel(out):
    out[...] = jnp.zeros_like(out)


def seed_kernel(seed_class, seed_mask, base):
    width, classes = base.shape
    kind = jnp.where(seed_mask[...] == 1, seed_class[...], -1)
    kind = jnp.transpose(jnp.broadcast_to(kind, (width, width)))
    for start in range(0, classes, width):
        slots = lax.broadcasted_iota(jnp.int32, (width, width), 1) + start
        base[:, start : start + width] = jnp.where(kind == slots, 1.0 - CARRY, 0.0)


def product(left, right, contract):
    return lax.dot_general(left, right, ((contract[:1], contract[1:]), ((), ())), preferred_element_type=jnp.float32)


def blocks_of(order, y_count, refs, i, j):
    z_count = len(order)
    sent, refs = refs[:z_count], refs[z_count:]
    strips = dict(zip([0] + others(z_count), sent[:1] + refs))
    from_core, halves = refs[z_count - 1], refs[z_count:]

    def back_block(k):
        if j > 0:
            return halves[j - 1][i, k]
        return sent[k][0, 0] if i == 0 else from_core[k, 0]

    back = jnp.concatenate([back_block(k) for k in order], axis=0)
    return back, jnp.concatenate([strips[k][i, j] for k in order], axis=1)


def ours_kernel(order, y_count, first, *refs):
    count = 2 * len(order) + y_count - 1
    blocks, pieces, outs = refs[:count], refs[count:-y_count], refs[-y_count:]
    pieces = pieces[:-1] if first else pieces
    values = jnp.concatenate([piece[...] for piece in pieces], axis=0)
    depth, classes = values.shape
    width = depth // len(order)
    ones = jnp.ones((SUBLANES, depth), jnp.bfloat16)
    for j, out in enumerate(outs):
        back, ahead = blocks_of(order, y_count, blocks, 0, j)
        out[:width, :] = product(back, values, (0, 0)) + product(ahead, values, (1, 0))
        if first:
            sums = product(ones, back, (1, 0)) + product(ones, ahead, (1, 1))
            back, ahead = blocks_of(order, y_count, blocks, 1, j)
            sums += product(ones, back, (1, 0)) + product(ones, ahead, (1, 1))
            out[width:, :] = jnp.concatenate([sums] * (classes // width), axis=1)


def theirs_kernel(order, y_count, wanted, first, *refs):
    count = 2 * len(order) + y_count - 1
    blocks, pieces, refs = refs[:count], refs[count : -2 * len(wanted)], refs[-2 * len(wanted) :]
    values = jnp.concatenate([piece[...] for piece in pieces], axis=0)
    width = values.shape[0] // len(order)
    for j, part, out in zip(wanted, refs[: len(wanted)], refs[len(wanted) :]):
        back, ahead = blocks_of(order, y_count, blocks, 1, j)
        total = part[:width, :] + product(back, values, (0, 0)) + product(ahead, values, (1, 0))
        out[:width, :] = total.astype(out.dtype)
        if first:
            sums = part[width:, :]
            if j > 0:
                sums = jnp.concatenate([sums] * 2, axis=0)
                high = sums.astype(jnp.bfloat16).astype(jnp.float32)
                middle = (sums - high).astype(jnp.bfloat16).astype(jnp.float32)
                row = lax.broadcasted_iota(jnp.int32, sums.shape, 0)
                sums = jnp.where(row == 0, high, jnp.where(row == 1, middle, sums - high - middle))
            out[width:, :] = sums.astype(out.dtype)


def on_device(affinity, block_live, labels, seed_class, seed_mask):
    stripe, sides, width = affinity.shape
    count = lax.axis_size("row")
    z_count, y_count = split_rows(count)
    classes = labels.shape[1]

    strip = jax.ShapeDtypeStruct((2, y_count, width, width), jnp.bfloat16)
    half = jax.ShapeDtypeStruct((2, z_count, width, width), jnp.bfloat16)
    sent = call(
        lambda *refs: prepare_kernel(z_count, y_count, *refs),
        [strip] * z_count,
        block_live.transpose(1, 2, 0),
        affinity.reshape(stripe * sides, width),
        call(lead_kernel, jax.ShapeDtypeStruct((SUBLANES, width), jnp.float32), flops=LEAD_FLOPS),
        smem=1,
    )
    other = jax.ShapeDtypeStruct((z_count, y_count, width, width), jnp.bfloat16)
    from_core = swap_cores(call(other_kernel, other, *sent))
    halves = call(lambda *refs: halves_kernel(z_count, *refs), [half] * (y_count - 1), *sent, from_core)
    halves = [swap_rows(x, j + 1) for j, x in enumerate(halves)]
    arrived = {k: swap_rows(sent[k], k * y_count) for k in others(z_count)}
    strips = [arrived[k] for k in others(z_count)]
    strips = [arrived[k] for k in others(z_count)]
    mark = guard(strips, STRIPS_FLOPS)
    blocks = [*sent, *strips, from_core, *halves]
    have, order, bit = [labels], [0], z_count // 2
    while bit:
        whole = have[0] if len(have) == 1 else join(have, PAIR_FLOPS)
        have = [whole, swap_rows(whole, bit * y_count)]
        order = order + [k ^ bit for k in order]
        bit //= 2
    base = call(
        seed_kernel,
        jax.ShapeDtypeStruct((width, classes), jnp.float32),
        seed_class.reshape(1, width),
        seed_mask.reshape(1, width),
    )

    current, degree = labels, None
    for step in range(ITERS):
        if step > 0:
            order = [0] + others_late(z_count)
            have = [current] + [swap_rows(current, k * y_count) for k in order[1:]]
        first = step == 0
        have = [join(have)] if first else [join(have[:-1]), join(have[-1:], LAST_FLOPS)]
        extra = SUBLANES if first else 0
        part = jax.ShapeDtypeStruct((width + extra, classes), jnp.float32)
        send = jax.ShapeDtypeStruct((width + 2 * extra, classes), jnp.bfloat16)
        parts = call(
            lambda *refs: ours_kernel(order, y_count, first, *refs),
            [part] * y_count,
            *blocks,
            *have,
            *([mark] if first else []),
            flops=OURS_FLOPS if first else 0,
        )
        have = [swap_cores(x) for x in have]
        wanted = range(1, y_count)
        sends = call(
            lambda *refs: theirs_kernel(order, y_count, wanted, first, *refs), [send] * (y_count - 1), *blocks, *have, *parts[1:]
        )
        (total,) = call(lambda *refs: theirs_kernel(order, y_count, [0], first, *refs), [part], *blocks, *have, parts[0])
        sends = [swap_rows(x, j + 1).astype(jnp.float32) for j, x in enumerate(sends)]
        spread = sum((x[:width] for x in sends), total[:width])
        if first:
            sums = sum((x[width : width + 3, :width].sum(axis=0) for x in sends), total[width, :width])
            degree = 1.0 + 0.5 * sums[:, None]
        mixed = CARRY * (0.5 * spread + current.astype(jnp.float32)) / degree
        current = (mixed + base).astype(jnp.bfloat16)
    return current


def solution(mesh):
    return jax.shard_map(
        on_device,
        mesh=mesh,
        in_specs=(
            P(("groups", "col"), None, "row"),
            P(("groups", "col"), None, "row"),
            P(("groups", "col", "row"), None),
            P(("groups", "col", "row")),
            P(("groups", "col", "row")),
        ),
        out_specs=P(("groups", "col", "row"), None),
        check_vma=False,
    )
```

```python
import jax
import jax.numpy as jnp
from jax import lax
from jax.experimental import pallas as pl
from jax.experimental.pallas import tpu as pltpu
from jax.sharding import PartitionSpec as P

ITERS = 2
CARRY = 0.8
SUBLANES = 8
LANES = 128
LEAD_FLOPS = 2_000_000_000
PAIR_FLOPS = 4_000_000_000
STRIPS_FLOPS = 3_000_000_000
OURS_FLOPS = 3_000_000_000
LAST_FLOPS = 2_000_000_000
MIB = 1024 * 1024


def split_rows(count):
    inner = 1 << ((count.bit_length() - 1) // 2)
    return count // inner, inner


def swap_rows(value, shift):
    count = lax.axis_size("row")
    return lax.ppermute(value, "row", [(i, i ^ shift) for i in range(count)])


def swap_cores(value):
    return lax.ppermute(value, "col", [(0, 1), (1, 0)])


def call(kernel, out_shape, *operands, smem=0, flops=0):
    spaces = [pltpu.SMEM] * smem + [pltpu.VMEM] * (len(operands) - smem)
    size = sum(x.size * x.dtype.itemsize for x in (*operands, *jax.tree.leaves(out_shape)))
    return pl.pallas_call(
        kernel,
        out_shape=out_shape,
        in_specs=[pl.BlockSpec(memory_space=space) for space in spaces],
        out_specs=jax.tree.map(lambda _: pl.BlockSpec(memory_space=pltpu.VMEM), out_shape),
        compiler_params=pltpu.CompilerParams(vmem_limit_bytes=2 * size + 4 * MIB),
        cost_estimate=pl.CostEstimate(flops=flops, bytes_accessed=size, transcendentals=0),
    )(*operands)


def others(count):
    return list(range(1, count))


def others_late(count):
    half = count // 2
    return list(range(1, half)) + list(range(half + 1, count)) + [half]


def prepare_kernel(z_count, y_count, live, tile, labels, lead, *outs):
    strips = outs
    row, col = lax.axis_index("row"), lax.axis_index("col")
    z, y = lax.div(row, y_count), lax.rem(row, y_count)
    width = tile.shape[1]
    for k in range(z_count):
        for j in range(y_count):
            block = lax.bitwise_xor(z, k) * y_count + lax.bitwise_xor(y, j)
            rows = tile.at[pl.ds(pl.multiple_of(block * 2 * width, 2 * width), 2 * width)]
            for side in range(2):
                piece = rows[pl.ds(side, width, stride=2), :]
                keep = live[side, 0, block] == 1
                strips[k][lax.bitwise_xor(col, side), j] = jnp.where(keep, piece, jnp.zeros_like(piece))


def other_kernel(*refs):
    strips, out = refs[:-1], refs[-1]
    for k, strip in enumerate(strips):
        out[k] = strip[1]


def halves_kernel(z_count, *refs):
    strips, from_core, halves = refs[:z_count], refs[z_count], refs[z_count + 1 :]
    for j, half in enumerate(halves, 1):
        for k in range(z_count):
            half[0, k] = strips[k][0, j]
            half[1, k] = from_core[k, j]


def join_kernel(*refs):
    parts, out = refs[:-1], refs[-1]
    start = 0
    for part in parts:
        out[start : start + part.shape[0]] = part[...]
        start += part.shape[0]


def join(parts, flops=0):
    rows = sum(x.shape[0] for x in parts)
    return call(join_kernel, jax.ShapeDtypeStruct((rows,) + parts[0].shape[1:], parts[0].dtype), *parts, flops=flops)


def guard_kernel(*refs):
    refs[-1][...] = jnp.zeros_like(refs[-1])


def guard(parts, flops):
    return call(guard_kernel, jax.ShapeDtypeStruct((SUBLANES, LANES), jnp.float32), *parts, flops=flops)


def lead_kernel(out):
    out[...] = jnp.zeros_like(out)


def seed_kernel(seed_class, seed_mask, base):
    width, classes = base.shape
    kind = jnp.where(seed_mask[...] == 1, seed_class[...], -1)
    kind = jnp.transpose(jnp.broadcast_to(kind, (width, width)))
    for start in range(0, classes, width):
        slots = lax.broadcasted_iota(jnp.int32, (width, width), 1) + start
        base[:, start : start + width] = jnp.where(kind == slots, 1.0 - CARRY, 0.0)


def product(left, right, contract):
    return lax.dot_general(left, right, ((contract[:1], contract[1:]), ((), ())), preferred_element_type=jnp.float32)


def blocks_of(z_count, y_count, refs, i, j, order):
    sent, refs = refs[:z_count], refs[z_count:]
    strips = dict(zip([0] + others(z_count), sent[:1] + refs))
    from_core, halves = refs[z_count - 1], refs[z_count:]

    def back_block(k):
        if j > 0:
            return halves[j - 1][i, k]
        return sent[k][0, 0] if i == 0 else from_core[k, 0]

    back = jnp.concatenate([back_block(k) for k in order], axis=0)
    return back, jnp.concatenate([strips[k][i, j] for k in order], axis=1)


def ours_kernel(z_count, y_count, order, first, *refs):
    count = 2 * z_count + y_count - 1
    blocks, pieces, outs = refs[:count], refs[count:-y_count], refs[-y_count:]
    pieces = pieces[:-1] if first else pieces
    values = jnp.concatenate([piece[...] for piece in pieces], axis=0)
    depth, classes = values.shape
    width = depth // z_count
    ones = jnp.ones((SUBLANES, depth), jnp.bfloat16)
    for j, out in enumerate(outs):
        back, ahead = blocks_of(z_count, y_count, blocks, 0, j, order)
        out[:width, :] = product(back, values, (0, 0)) + product(ahead, values, (1, 0))
        if first:
            sums = product(ones, back, (1, 0)) + product(ones, ahead, (1, 1))
            back, ahead = blocks_of(z_count, y_count, blocks, 1, j, order)
            sums += product(ones, back, (1, 0)) + product(ones, ahead, (1, 1))
            out[width:, :] = jnp.concatenate([sums] * (classes // width), axis=1)


def theirs_kernel(z_count, y_count, order, wanted, first, *refs):
    count = 2 * z_count + y_count - 1
    blocks, piece, parts, outs = refs[:count], refs[count], refs[count + 1 : -len(wanted)], refs[-len(wanted) :]
    values = piece[...]
    width = values.shape[0] // len(order)
    for j, part, out in zip(wanted, parts, outs):
        back, ahead = blocks_of(z_count, y_count, blocks, 1, j, order)
        total = part[:width, :] + product(back, values, (0, 0)) + product(ahead, values, (1, 0))
        out[:width, :] = total.astype(out.dtype)
        if first:
            sums = part[width:, :]
            if j > 0:
                sums = jnp.concatenate([sums] * 2, axis=0)
                high = sums.astype(jnp.bfloat16).astype(jnp.float32)
                middle = (sums - high).astype(jnp.bfloat16).astype(jnp.float32)
                row = lax.broadcasted_iota(jnp.int32, sums.shape, 0)
                sums = jnp.where(row == 0, high, jnp.where(row == 1, middle, sums - high - middle))
            out[width:, :] = sums.astype(out.dtype)


def on_device(affinity, block_live, labels, seed_class, seed_mask):
    stripe, sides, width = affinity.shape
    count = lax.axis_size("row")
    z_count, y_count = split_rows(count)
    classes = labels.shape[1]

    strip = jax.ShapeDtypeStruct((2, y_count, width, width), jnp.bfloat16)
    half = jax.ShapeDtypeStruct((2, z_count, width, width), jnp.bfloat16)
    sent = call(
        lambda *refs: prepare_kernel(z_count, y_count, *refs),
        [strip] * z_count,
        block_live.transpose(1, 2, 0),
        affinity.reshape(stripe * sides, width),
        labels,
        call(lead_kernel, jax.ShapeDtypeStruct((SUBLANES, width), jnp.float32), flops=LEAD_FLOPS),
        smem=1,
    )
    other = jax.ShapeDtypeStruct((z_count, y_count, width, width), jnp.bfloat16)
    from_core = swap_cores(call(other_kernel, other, *sent))
    halves = call(lambda *refs: halves_kernel(z_count, *refs), [half] * (y_count - 1), *sent, from_core)
    halves = [swap_rows(x, j + 1) for j, x in enumerate(halves)]
    arrived = {k: swap_rows(sent[k], k * y_count) for k in others(z_count)}
    strips = [arrived[k] for k in others(z_count)]
    strips = [arrived[k] for k in others(z_count)]
    mark = guard(strips, STRIPS_FLOPS)
    blocks = [*sent, *strips, from_core, *halves]
    have, order, bit = [labels], [0], z_count // 2
    while bit:
        whole = have[0] if len(have) == 1 else join(have, PAIR_FLOPS)
        have = [whole, swap_rows(whole, bit * y_count)]
        order = order + [k ^ bit for k in order]
        bit //= 2
    base = call(
        seed_kernel,
        jax.ShapeDtypeStruct((width, classes), jnp.float32),
        seed_class.reshape(1, width),
        seed_mask.reshape(1, width),
    )

    current, degree = labels, None
    for step in range(ITERS):
        if step > 0:
            order = [0] + others_late(z_count)
            have = [current] + [swap_rows(current, k * y_count) for k in order[1:]]
        first = step == 0
        have = [join(have)] if first else [join(have[:-1]), join(have[-1:], LAST_FLOPS)]
        extra = SUBLANES if first else 0
        part = jax.ShapeDtypeStruct((width + extra, classes), jnp.float32)
        send = jax.ShapeDtypeStruct((width + 2 * extra, classes), jnp.bfloat16)
        parts = call(
            lambda *refs: ours_kernel(z_count, y_count, order, first, *refs),
            [part] * y_count,
            *blocks,
            *have,
            *([mark] if first else []),
            flops=OURS_FLOPS if first else 0,
        )

        def add_theirs(values, order, wanted, shape):
            return call(
                lambda *refs: theirs_kernel(z_count, y_count, order, wanted, first, *refs),
                [shape] * len(wanted),
                *blocks,
                values,
                *[parts[j] for j in wanted],
            )

        *early, last = [swap_cores(x) for x in have]
        if early:
            parts = add_theirs(early[0], order[:-1], range(y_count), part)
        ending = order[-1:] if early else order
        sends = add_theirs(last, ending, range(1, y_count), send)
        (total,) = add_theirs(last, ending, range(1), part)
        sends = [swap_rows(x, j + 1).astype(jnp.float32) for j, x in enumerate(sends)]
        spread = sum((x[:width] for x in sends), total[:width])
        if first:
            sums = sum((x[width : width + 3, :width].sum(axis=0) for x in sends), total[width, :width])
            degree = 1.0 + 0.5 * sums[:, None]
        mixed = CARRY * (0.5 * spread + current.astype(jnp.float32)) / degree
        current = (mixed + base).astype(jnp.bfloat16)
    return current


def solution(mesh):
    return jax.shard_map(
        on_device,
        mesh=mesh,
        in_specs=(
            P(("groups", "col"), None, "row"),
            P(("groups", "col"), None, "row"),
            P(("groups", "col", "row"), None),
            P(("groups", "col", "row")),
            P(("groups", "col", "row")),
        ),
        out_specs=P(("groups", "col", "row"), None),
        check_vma=False,
    )
```

```python
import jax
import jax.numpy as jnp
from jax import lax
from jax.experimental import pallas as pl
from jax.experimental.pallas import tpu as pltpu
from jax.sharding import PartitionSpec as P

ITERS = 2
CARRY = 0.8
SUBLANES = 8
LANES = 128
LEAD_FLOPS = 2_000_000_000
PAIR_FLOPS = 4_000_000_000
STRIPS_FLOPS = 3_000_000_000
OURS_FLOPS = 3_000_000_000
LAST_FLOPS = 2_000_000_000
MIB = 1024 * 1024


def split_rows(count):
    inner = 1 << ((count.bit_length() - 1) // 2)
    return count // inner, inner


def swap_rows(value, shift):
    count = lax.axis_size("row")
    return lax.ppermute(value, "row", [(i, i ^ shift) for i in range(count)])


def swap_cores(value):
    return lax.ppermute(value, "col", [(0, 1), (1, 0)])


def call(kernel, out_shape, *operands, smem=0, flops=0):
    spaces = [pltpu.SMEM] * smem + [pltpu.VMEM] * (len(operands) - smem)
    size = sum(x.size * x.dtype.itemsize for x in (*operands, *jax.tree.leaves(out_shape)))
    return pl.pallas_call(
        kernel,
        out_shape=out_shape,
        in_specs=[pl.BlockSpec(memory_space=space) for space in spaces],
        out_specs=jax.tree.map(lambda _: pl.BlockSpec(memory_space=pltpu.VMEM), out_shape),
        compiler_params=pltpu.CompilerParams(vmem_limit_bytes=2 * size + 4 * MIB),
        cost_estimate=pl.CostEstimate(flops=flops, bytes_accessed=size, transcendentals=0),
    )(*operands)


def others(count):
    return list(range(1, count))


def others_late(count):
    half = count // 2
    return list(range(1, half)) + list(range(half + 1, count)) + [half]


def prepare_kernel(z_count, y_count, live, tile, labels, lead, *outs):
    strips = outs
    row, col = lax.axis_index("row"), lax.axis_index("col")
    z, y = lax.div(row, y_count), lax.rem(row, y_count)
    width = tile.shape[1]
    for k in range(z_count):
        for j in range(y_count):
            block = lax.bitwise_xor(z, k) * y_count + lax.bitwise_xor(y, j)
            rows = tile.at[pl.ds(pl.multiple_of(block * 2 * width, 2 * width), 2 * width)]
            for side in range(2):
                piece = rows[pl.ds(side, width, stride=2), :]
                keep = live[side, 0, block] == 1
                strips[k][lax.bitwise_xor(col, side), j] = jnp.where(keep, piece, jnp.zeros_like(piece))


def other_kernel(*refs):
    strips, out = refs[:-1], refs[-1]
    for k, strip in enumerate(strips):
        out[k] = strip[1]


def halves_kernel(z_count, *refs):
    strips, from_core, halves = refs[:z_count], refs[z_count], refs[z_count + 1 :]
    for j, half in enumerate(halves, 1):
        for k in range(z_count):
            half[0, k] = strips[k][0, j]
            half[1, k] = from_core[k, j]


def join_kernel(*refs):
    parts, out = refs[:-1], refs[-1]
    start = 0
    for part in parts:
        out[start : start + part.shape[0]] = part[...]
        start += part.shape[0]


def join(parts, flops=0):
    rows = sum(x.shape[0] for x in parts)
    return call(join_kernel, jax.ShapeDtypeStruct((rows,) + parts[0].shape[1:], parts[0].dtype), *parts, flops=flops)


def guard_kernel(*refs):
    refs[-1][...] = jnp.zeros_like(refs[-1])


def guard(parts, flops):
    return call(guard_kernel, jax.ShapeDtypeStruct((SUBLANES, LANES), jnp.float32), *parts, flops=flops)


def lead_kernel(out):
    out[...] = jnp.zeros_like(out)


def seed_kernel(seed_class, seed_mask, base):
    width, classes = base.shape
    kind = jnp.where(seed_mask[...] == 1, seed_class[...], -1)
    kind = jnp.transpose(jnp.broadcast_to(kind, (width, width)))
    for start in range(0, classes, width):
        slots = lax.broadcasted_iota(jnp.int32, (width, width), 1) + start
        base[:, start : start + width] = jnp.where(kind == slots, 1.0 - CARRY, 0.0)


def product(left, right, contract):
    return lax.dot_general(left, right, ((contract[:1], contract[1:]), ((), ())), preferred_element_type=jnp.float32)


def blocks_of(order, y_count, refs, i, j):
    z_count = len(order)
    sent, refs = refs[:z_count], refs[z_count:]
    strips = dict(zip([0] + others(z_count), sent[:1] + refs))
    from_core, halves = refs[z_count - 1], refs[z_count:]

    def back_block(k):
        if j > 0:
            return halves[j - 1][i, k]
        return sent[k][0, 0] if i == 0 else from_core[k, 0]

    back = jnp.concatenate([back_block(k) for k in order], axis=0)
    return back, jnp.concatenate([strips[k][i, j] for k in order], axis=1)


def ours_kernel(order, y_count, first, *refs):
    count = 2 * len(order) + y_count - 1
    blocks, pieces, outs = refs[:count], refs[count:-y_count], refs[-y_count:]
    pieces = pieces[:-1] if first else pieces
    values = jnp.concatenate([piece[...] for piece in pieces], axis=0)
    depth, classes = values.shape
    width = depth // len(order)
    ones = jnp.ones((SUBLANES, depth), jnp.bfloat16)
    for j, out in enumerate(outs):
        back, ahead = blocks_of(order, y_count, blocks, 0, j)
        out[:width, :] = product(back, values, (0, 0)) + product(ahead, values, (1, 0))
        if first:
            sums = product(ones, back, (1, 0)) + product(ones, ahead, (1, 1))
            back, ahead = blocks_of(order, y_count, blocks, 1, j)
            sums += product(ones, back, (1, 0)) + product(ones, ahead, (1, 1))
            sums = jnp.concatenate([sums] * (classes // width), axis=1)
            if j > 0:
                sums = jnp.concatenate([sums] * 2, axis=0)
                high = sums.astype(jnp.bfloat16).astype(jnp.float32)
                middle = (sums - high).astype(jnp.bfloat16).astype(jnp.float32)
                row = lax.broadcasted_iota(jnp.int32, sums.shape, 0)
                sums = jnp.where(row == 0, high, jnp.where(row == 1, middle, sums - high - middle))
            out[width:, :] = sums


def theirs_kernel(order, y_count, wanted, first, *refs):
    count = 2 * len(order) + y_count - 1
    blocks, pieces, refs = refs[:count], refs[count : -2 * len(wanted)], refs[-2 * len(wanted) :]
    values = jnp.concatenate([piece[...] for piece in pieces], axis=0)
    width = values.shape[0] // len(order)
    for j, part, out in zip(wanted, refs[: len(wanted)], refs[len(wanted) :]):
        back, ahead = blocks_of(order, y_count, blocks, 1, j)
        total = part[:width, :] + product(back, values, (0, 0)) + product(ahead, values, (1, 0))
        out[:width, :] = total.astype(out.dtype)
        if first:
            out[width:, :] = part[width:, :].astype(out.dtype)


def on_device(affinity, block_live, labels, seed_class, seed_mask):
    stripe, sides, width = affinity.shape
    count = lax.axis_size("row")
    z_count, y_count = split_rows(count)
    classes = labels.shape[1]

    strip = jax.ShapeDtypeStruct((2, y_count, width, width), jnp.bfloat16)
    half = jax.ShapeDtypeStruct((2, z_count, width, width), jnp.bfloat16)
    sent = call(
        lambda *refs: prepare_kernel(z_count, y_count, *refs),
        [strip] * z_count,
        block_live.transpose(1, 2, 0),
        affinity.reshape(stripe * sides, width),
        labels,
        call(lead_kernel, jax.ShapeDtypeStruct((SUBLANES, width), jnp.float32), flops=LEAD_FLOPS),
        smem=1,
    )
    other = jax.ShapeDtypeStruct((z_count, y_count, width, width), jnp.bfloat16)
    from_core = swap_cores(call(other_kernel, other, *sent))
    halves = call(lambda *refs: halves_kernel(z_count, *refs), [half] * (y_count - 1), *sent, from_core)
    halves = [swap_rows(x, j + 1) for j, x in enumerate(halves)]
    arrived = {k: swap_rows(sent[k], k * y_count) for k in others(z_count)}
    strips = [arrived[k] for k in others(z_count)]
    strips = [arrived[k] for k in others(z_count)]
    mark = guard(strips, STRIPS_FLOPS)
    blocks = [*sent, *strips, from_core, *halves]
    have, order, bit = [labels], [0], z_count // 2
    while bit:
        whole = have[0] if len(have) == 1 else join(have, PAIR_FLOPS)
        have = [whole, swap_rows(whole, bit * y_count)]
        order = order + [k ^ bit for k in order]
        bit //= 2
    base = call(
        seed_kernel,
        jax.ShapeDtypeStruct((width, classes), jnp.float32),
        seed_class.reshape(1, width),
        seed_mask.reshape(1, width),
    )

    current, degree = labels, None
    for step in range(ITERS):
        if step > 0:
            order = [0] + others_late(z_count)
            have = [current] + [swap_rows(current, k * y_count) for k in order[1:]]
        first = step == 0
        have = [join(have)] if first else [join(have[:-1]), join(have[-1:], LAST_FLOPS)]
        extra = SUBLANES if first else 0
        part = jax.ShapeDtypeStruct((width + extra, classes), jnp.float32)
        send = jax.ShapeDtypeStruct((width + 2 * extra, classes), jnp.bfloat16)
        parts = call(
            lambda *refs: ours_kernel(order, y_count, first, *refs),
            [part] + [jax.ShapeDtypeStruct(send.shape, jnp.float32)] * (y_count - 1),
            *blocks,
            *have,
            *([mark] if first else []),
            flops=OURS_FLOPS if first else 0,
        )
        have = [swap_cores(x) for x in have]
        wanted = range(1, y_count)
        sends = call(
            lambda *refs: theirs_kernel(order, y_count, wanted, first, *refs), [send] * (y_count - 1), *blocks, *have, *parts[1:]
        )
        (total,) = call(lambda *refs: theirs_kernel(order, y_count, [0], first, *refs), [part], *blocks, *have, parts[0])
        sends = [swap_rows(x, j + 1).astype(jnp.float32) for j, x in enumerate(sends)]
        spread = sum((x[:width] for x in sends), total[:width])
        if first:
            sums = sum((x[width : width + 3, :width].sum(axis=0) for x in sends), total[width, :width])
            degree = 1.0 + 0.5 * sums[:, None]
        mixed = CARRY * (0.5 * spread + current.astype(jnp.float32)) / degree
        current = (mixed + base).astype(jnp.bfloat16)
    return current


def solution(mesh):
    return jax.shard_map(
        on_device,
        mesh=mesh,
        in_specs=(
            P(("groups", "col"), None, "row"),
            P(("groups", "col"), None, "row"),
            P(("groups", "col", "row"), None),
            P(("groups", "col", "row")),
            P(("groups", "col", "row")),
        ),
        out_specs=P(("groups", "col", "row"), None),
        check_vma=False,
    )
```

```python
import jax
import jax.numpy as jnp
from jax import lax
from jax.experimental import pallas as pl
from jax.experimental.pallas import tpu as pltpu
from jax.sharding import PartitionSpec as P

ITERS = 2
CARRY = 0.8
SUBLANES = 8
LANES = 128
LEAD_FLOPS = 2_000_000_000
PAIR_FLOPS = 4_000_000_000
STRIPS_FLOPS = 3_000_000_000
OURS_FLOPS = 3_000_000_000
EARLY_FLOPS = 3_000_000_000
LAST_FLOPS = 2_000_000_000
MIB = 1024 * 1024


def split_rows(count):
    inner = 1 << ((count.bit_length() - 1) // 2)
    return count // inner, inner


def swap_rows(value, shift):
    count = lax.axis_size("row")
    return lax.ppermute(value, "row", [(i, i ^ shift) for i in range(count)])


def swap_cores(value):
    return lax.ppermute(value, "col", [(0, 1), (1, 0)])


def call(kernel, out_shape, *operands, smem=0, flops=0):
    spaces = [pltpu.SMEM] * smem + [pltpu.VMEM] * (len(operands) - smem)
    size = sum(x.size * x.dtype.itemsize for x in (*operands, *jax.tree.leaves(out_shape)))
    return pl.pallas_call(
        kernel,
        out_shape=out_shape,
        in_specs=[pl.BlockSpec(memory_space=space) for space in spaces],
        out_specs=jax.tree.map(lambda _: pl.BlockSpec(memory_space=pltpu.VMEM), out_shape),
        compiler_params=pltpu.CompilerParams(vmem_limit_bytes=2 * size + 4 * MIB),
        cost_estimate=pl.CostEstimate(flops=flops, bytes_accessed=size, transcendentals=0),
    )(*operands)


def others(count):
    return list(range(1, count))


def others_late(count):
    half = count // 2
    return list(range(1, half)) + list(range(half + 1, count)) + [half]


def prepare_kernel(z_count, y_count, live, tile, labels, lead, *outs):
    strips = outs
    row, col = lax.axis_index("row"), lax.axis_index("col")
    z, y = lax.div(row, y_count), lax.rem(row, y_count)
    width = tile.shape[1]
    for k in range(z_count):
        for j in range(y_count):
            block = lax.bitwise_xor(z, k) * y_count + lax.bitwise_xor(y, j)
            rows = tile.at[pl.ds(pl.multiple_of(block * 2 * width, 2 * width), 2 * width)]
            for side in range(2):
                piece = rows[pl.ds(side, width, stride=2), :]
                keep = live[side, 0, block] == 1
                strips[k][lax.bitwise_xor(col, side), j] = jnp.where(keep, piece, jnp.zeros_like(piece))


def other_kernel(*refs):
    strips, out = refs[:-1], refs[-1]
    for k, strip in enumerate(strips):
        out[k] = strip[1]


def halves_kernel(z_count, *refs):
    strips, from_core, halves = refs[:z_count], refs[z_count], refs[z_count + 1 :]
    for j, half in enumerate(halves, 1):
        for k in range(z_count):
            half[0, k] = strips[k][0, j]
            half[1, k] = from_core[k, j]


def join_kernel(*refs):
    parts, out = refs[:-1], refs[-1]
    start = 0
    for part in parts:
        out[start : start + part.shape[0]] = part[...]
        start += part.shape[0]


def join(parts, flops=0):
    rows = sum(x.shape[0] for x in parts)
    return call(join_kernel, jax.ShapeDtypeStruct((rows,) + parts[0].shape[1:], parts[0].dtype), *parts, flops=flops)


def behind_kernel(value, *refs):
    refs[-1][...] = value[...]


def guard_kernel(*refs):
    refs[-1][...] = jnp.zeros_like(refs[-1])


def guard(parts, flops):
    return call(guard_kernel, jax.ShapeDtypeStruct((SUBLANES, LANES), jnp.float32), *parts, flops=flops)


def lead_kernel(out):
    out[...] = jnp.zeros_like(out)


def seed_kernel(seed_class, seed_mask, base):
    width, classes = base.shape
    kind = jnp.where(seed_mask[...] == 1, seed_class[...], -1)
    kind = jnp.transpose(jnp.broadcast_to(kind, (width, width)))
    for start in range(0, classes, width):
        slots = lax.broadcasted_iota(jnp.int32, (width, width), 1) + start
        base[:, start : start + width] = jnp.where(kind == slots, 1.0 - CARRY, 0.0)


def product(left, right, contract):
    return lax.dot_general(left, right, ((contract[:1], contract[1:]), ((), ())), preferred_element_type=jnp.float32)


def blocks_of(z_count, y_count, refs, i, j, order):
    sent, refs = refs[:z_count], refs[z_count:]
    strips = dict(zip([0] + others(z_count), sent[:1] + refs))
    from_core, halves = refs[z_count - 1], refs[z_count:]

    def back_block(k):
        if j > 0:
            return halves[j - 1][i, k]
        return sent[k][0, 0] if i == 0 else from_core[k, 0]

    back = jnp.concatenate([back_block(k) for k in order], axis=0)
    return back, jnp.concatenate([strips[k][i, j] for k in order], axis=1)


def ours_kernel(z_count, y_count, order, first, *refs):
    count = 2 * z_count + y_count - 1
    blocks, pieces, outs = refs[:count], refs[count:-y_count], refs[-y_count:]
    pieces = pieces[:-1] if first else pieces
    values = jnp.concatenate([piece[...] for piece in pieces], axis=0)
    depth, classes = values.shape
    width = depth // z_count
    ones = jnp.ones((SUBLANES, depth), jnp.bfloat16)
    for j, out in enumerate(outs):
        back, ahead = blocks_of(z_count, y_count, blocks, 0, j, order)
        out[:width, :] = product(back, values, (0, 0)) + product(ahead, values, (1, 0))
        if first:
            sums = product(ones, back, (1, 0)) + product(ones, ahead, (1, 1))
            back, ahead = blocks_of(z_count, y_count, blocks, 1, j, order)
            sums += product(ones, back, (1, 0)) + product(ones, ahead, (1, 1))
            out[width:, :] = jnp.concatenate([sums] * (classes // width), axis=1)


def theirs_kernel(z_count, y_count, order, wanted, first, last, *refs):
    count = 2 * z_count + y_count - 1
    blocks, piece, parts, outs = refs[:count], refs[count], refs[count + 1 : -len(wanted)], refs[-len(wanted) :]
    values = piece[...]
    width = values.shape[0] // len(order)
    for j, part, out in zip(wanted, parts, outs):
        back, ahead = blocks_of(z_count, y_count, blocks, 1, j, order)
        total = part[:width, :] + product(back, values, (0, 0)) + product(ahead, values, (1, 0))
        out[:width, :] = total.astype(out.dtype)
        if first:
            sums = part[width:, :]
            if j > 0 and last:
                sums = jnp.concatenate([sums] * 2, axis=0)
                high = sums.astype(jnp.bfloat16).astype(jnp.float32)
                middle = (sums - high).astype(jnp.bfloat16).astype(jnp.float32)
                row = lax.broadcasted_iota(jnp.int32, sums.shape, 0)
                sums = jnp.where(row == 0, high, jnp.where(row == 1, middle, sums - high - middle))
            out[width:, :] = sums.astype(out.dtype)


def on_device(affinity, block_live, labels, seed_class, seed_mask):
    stripe, sides, width = affinity.shape
    count = lax.axis_size("row")
    z_count, y_count = split_rows(count)
    classes = labels.shape[1]

    strip = jax.ShapeDtypeStruct((2, y_count, width, width), jnp.bfloat16)
    half = jax.ShapeDtypeStruct((2, z_count, width, width), jnp.bfloat16)
    sent = call(
        lambda *refs: prepare_kernel(z_count, y_count, *refs),
        [strip] * z_count,
        block_live.transpose(1, 2, 0),
        affinity.reshape(stripe * sides, width),
        labels,
        call(lead_kernel, jax.ShapeDtypeStruct((SUBLANES, width), jnp.float32), flops=LEAD_FLOPS),
        smem=1,
    )
    other = jax.ShapeDtypeStruct((z_count, y_count, width, width), jnp.bfloat16)
    from_core = swap_cores(call(other_kernel, other, *sent))
    halves = call(lambda *refs: halves_kernel(z_count, *refs), [half] * (y_count - 1), *sent, from_core)
    ready = halves
    halves = [swap_rows(x, j + 1) for j, x in enumerate(halves)]
    arrived = {k: swap_rows(sent[k], k * y_count) for k in others(z_count)}
    strips = [arrived[k] for k in others(z_count)]
    strips = [arrived[k] for k in others(z_count)]
    mark = guard(strips, STRIPS_FLOPS)
    blocks = [*sent, *strips, from_core, *halves]
    have, order, bit = [labels], [0], z_count // 2
    while bit:
        whole = have[0] if len(have) == 1 else join(have, PAIR_FLOPS)
        have = [whole, swap_rows(whole, bit * y_count)]
        order = order + [k ^ bit for k in order]
        bit //= 2
    base = call(
        seed_kernel,
        jax.ShapeDtypeStruct((width, classes), jnp.float32),
        seed_class.reshape(1, width),
        seed_mask.reshape(1, width),
    )

    current, degree = labels, None
    for step in range(ITERS):
        if step > 0:
            order = [0] + others_late(z_count)
            have = [current] + [swap_rows(current, k * y_count) for k in order[1:]]
        first = step == 0
        have = have if first else [join(have[:-1]), join(have[-1:], LAST_FLOPS)]
        extra = SUBLANES if first else 0
        part = jax.ShapeDtypeStruct((width + extra, classes), jnp.float32)
        send = jax.ShapeDtypeStruct((width + 2 * extra, classes), jnp.bfloat16)
        parts = call(
            lambda *refs: ours_kernel(z_count, y_count, order, first, *refs),
            [part] * y_count,
            *blocks,
            *have,
            *([mark] if first else []),
            flops=OURS_FLOPS if first else 0,
        )

        def add_theirs(values, order, wanted, last, shape, flops=0):
            return call(
                lambda *refs: theirs_kernel(z_count, y_count, order, wanted, first, last, *refs),
                [shape] * len(wanted),
                *blocks,
                values,
                *[parts[j] for j in wanted],
                flops=flops,
            )

        early = have[0]
        if first:
            early = call(behind_kernel, jax.ShapeDtypeStruct(early.shape, early.dtype), early, arrived[1], *ready)
        early, last = swap_cores(early), swap_cores(have[1])
        cut = early.shape[0] // width
        parts = add_theirs(early, order[:cut], range(y_count), False, part, EARLY_FLOPS if first else 0)
        sends = add_theirs(last, order[cut:], range(1, y_count), True, send)
        (total,) = add_theirs(last, order[cut:], range(1), True, part)
        sends = [swap_rows(x, j + 1).astype(jnp.float32) for j, x in enumerate(sends)]
        spread = sum((x[:width] for x in sends), total[:width])
        if first:
            sums = sum((x[width : width + 3, :width].sum(axis=0) for x in sends), total[width, :width])
            degree = 1.0 + 0.5 * sums[:, None]
        mixed = CARRY * (0.5 * spread + current.astype(jnp.float32)) / degree
        current = (mixed + base).astype(jnp.bfloat16)
    return current


def solution(mesh):
    return jax.shard_map(
        on_device,
        mesh=mesh,
        in_specs=(
            P(("groups", "col"), None, "row"),
            P(("groups", "col"), None, "row"),
            P(("groups", "col", "row"), None),
            P(("groups", "col", "row")),
            P(("groups", "col", "row")),
        ),
        out_specs=P(("groups", "col", "row"), None),
        check_vma=False,
    )
```

```python
import jax
import jax.numpy as jnp
from jax import lax
from jax.experimental import pallas as pl
from jax.experimental.pallas import tpu as pltpu
from jax.sharding import PartitionSpec as P

ITERS = 2
CARRY = 0.8
SUBLANES = 8
LANES = 128
LEAD_FLOPS = 2_000_000_000
PAIR_FLOPS = 4_000_000_000
STRIPS_FLOPS = 3_000_000_000
OURS_FLOPS = 3_000_000_000
LAST_FLOPS = 2_000_000_000
MIB = 1024 * 1024


def split_rows(count):
    inner = 1 << ((count.bit_length() - 1) // 2)
    return count // inner, inner


def swap_rows(value, shift):
    count = lax.axis_size("row")
    return lax.ppermute(value, "row", [(i, i ^ shift) for i in range(count)])


def swap_cores(value):
    return lax.ppermute(value, "col", [(0, 1), (1, 0)])


def call(kernel, out_shape, *operands, smem=0, flops=0):
    spaces = [pltpu.SMEM] * smem + [pltpu.VMEM] * (len(operands) - smem)
    size = sum(x.size * x.dtype.itemsize for x in (*operands, *jax.tree.leaves(out_shape)))
    return pl.pallas_call(
        kernel,
        out_shape=out_shape,
        in_specs=[pl.BlockSpec(memory_space=space) for space in spaces],
        out_specs=jax.tree.map(lambda _: pl.BlockSpec(memory_space=pltpu.VMEM), out_shape),
        compiler_params=pltpu.CompilerParams(vmem_limit_bytes=2 * size + 4 * MIB),
        cost_estimate=pl.CostEstimate(flops=flops, bytes_accessed=size, transcendentals=0),
    )(*operands)


def others(count):
    return list(range(1, count))


def others_late(count):
    half = count // 2
    return list(range(1, half)) + list(range(half + 1, count)) + [half]


def prepare_kernel(z_count, y_count, live, tile, lead, *outs):
    strips = outs
    row, col = lax.axis_index("row"), lax.axis_index("col")
    z, y = lax.div(row, y_count), lax.rem(row, y_count)
    width = tile.shape[1]
    for k in range(z_count):
        for j in range(y_count):
            block = lax.bitwise_xor(z, k) * y_count + lax.bitwise_xor(y, j)
            rows = tile.at[pl.ds(pl.multiple_of(block * 2 * width, 2 * width), 2 * width)]
            for side in range(2):
                piece = rows[pl.ds(side, width, stride=2), :]
                keep = live[side, 0, block] == 1
                strips[k][lax.bitwise_xor(col, side), j] = jnp.where(keep, piece, jnp.zeros_like(piece))


def other_kernel(*refs):
    strips, out = refs[:-1], refs[-1]
    for k, strip in enumerate(strips):
        out[k] = strip[1]


def halves_kernel(z_count, *refs):
    strips, from_core, halves = refs[:z_count], refs[z_count], refs[z_count + 1 :]
    for j, half in enumerate(halves, 1):
        for k in range(z_count):
            half[0, k] = strips[k][0, j]
            half[1, k] = from_core[k, j]


def join_kernel(*refs):
    parts, out = refs[:-1], refs[-1]
    start = 0
    for part in parts:
        out[start : start + part.shape[0]] = part[...]
        start += part.shape[0]


def join(parts, flops=0):
    rows = sum(x.shape[0] for x in parts)
    return call(join_kernel, jax.ShapeDtypeStruct((rows,) + parts[0].shape[1:], parts[0].dtype), *parts, flops=flops)


def guard_kernel(*refs):
    refs[-1][...] = jnp.zeros_like(refs[-1])


def guard(parts, flops):
    return call(guard_kernel, jax.ShapeDtypeStruct((SUBLANES, LANES), jnp.float32), *parts, flops=flops)


def lead_kernel(out):
    out[...] = jnp.zeros_like(out)


def seed_kernel(seed_class, seed_mask, base):
    width, classes = base.shape
    kind = jnp.where(seed_mask[...] == 1, seed_class[...], -1)
    kind = jnp.transpose(jnp.broadcast_to(kind, (width, width)))
    for start in range(0, classes, width):
        slots = lax.broadcasted_iota(jnp.int32, (width, width), 1) + start
        base[:, start : start + width] = jnp.where(kind == slots, 1.0 - CARRY, 0.0)


def product(left, right, contract):
    return lax.dot_general(left, right, ((contract[:1], contract[1:]), ((), ())), preferred_element_type=jnp.float32)


def blocks_of(order, y_count, refs, i, j):
    z_count = len(order)
    sent, refs = refs[:z_count], refs[z_count:]
    strips = dict(zip([0] + others(z_count), sent[:1] + refs))
    from_core, halves = refs[z_count - 1], refs[z_count:]

    def back_block(k):
        if j > 0:
            return halves[j - 1][i, k]
        return sent[k][0, 0] if i == 0 else from_core[k, 0]

    back = jnp.concatenate([back_block(k) for k in order], axis=0)
    return back, jnp.concatenate([strips[k][i, j] for k in order], axis=1)


def ours_kernel(order, y_count, first, *refs):
    count = 2 * len(order) + y_count - 1
    blocks, pieces, outs = refs[:count], refs[count:-y_count], refs[-y_count:]
    pieces = pieces[:-1] if first else pieces
    values = jnp.concatenate([piece[...] for piece in pieces], axis=0)
    depth, classes = values.shape
    width = depth // len(order)
    ones = jnp.ones((SUBLANES, depth), jnp.bfloat16)
    for j, out in enumerate(outs):
        back, ahead = blocks_of(order, y_count, blocks, 0, j)
        out[:width, :] = product(back, values, (0, 0)) + product(ahead, values, (1, 0))
        if first:
            sums = product(ones, back, (1, 0)) + product(ones, ahead, (1, 1))
            back, ahead = blocks_of(order, y_count, blocks, 1, j)
            sums += product(ones, back, (1, 0)) + product(ones, ahead, (1, 1))
            out[width:, :] = jnp.concatenate([sums] * (classes // width), axis=1)


def theirs_kernel(order, y_count, wanted, first, *refs):
    count = 2 * len(order) + y_count - 1
    blocks, pieces, refs = refs[:count], refs[count : -2 * len(wanted)], refs[-2 * len(wanted) :]
    values = jnp.concatenate([piece[...] for piece in pieces], axis=0)
    width = values.shape[0] // len(order)
    for j, part, out in zip(wanted, refs[: len(wanted)], refs[len(wanted) :]):
        back, ahead = blocks_of(order, y_count, blocks, 1, j)
        total = part[:width, :] + product(back, values, (0, 0)) + product(ahead, values, (1, 0))
        out[:width, :] = total.astype(out.dtype)
        if first:
            sums = part[width:, :]
            if j > 0:
                sums = jnp.concatenate([sums] * 2, axis=0)
                high = sums.astype(jnp.bfloat16).astype(jnp.float32)
                middle = (sums - high).astype(jnp.bfloat16).astype(jnp.float32)
                row = lax.broadcasted_iota(jnp.int32, sums.shape, 0)
                sums = jnp.where(row == 0, high, jnp.where(row == 1, middle, sums - high - middle))
            out[width:, :] = sums.astype(out.dtype)


def on_device(affinity, block_live, labels, seed_class, seed_mask):
    stripe, sides, width = affinity.shape
    count = lax.axis_size("row")
    z_count, y_count = split_rows(count)
    classes = labels.shape[1]

    strip = jax.ShapeDtypeStruct((2, y_count, width, width), jnp.bfloat16)
    half = jax.ShapeDtypeStruct((2, z_count, width, width), jnp.bfloat16)
    sent = call(
        lambda *refs: prepare_kernel(z_count, y_count, *refs),
        [strip] * z_count,
        block_live.transpose(1, 2, 0),
        affinity.reshape(stripe * sides, width),
        call(lead_kernel, jax.ShapeDtypeStruct((SUBLANES, width), jnp.float32), flops=LEAD_FLOPS),
        smem=1,
    )
    other = jax.ShapeDtypeStruct((z_count, y_count, width, width), jnp.bfloat16)
    from_core = swap_cores(call(other_kernel, other, *sent))
    halves = call(lambda *refs: halves_kernel(z_count, *refs), [half] * (y_count - 1), *sent, from_core)
    halves = [swap_rows(x, j + 1) for j, x in enumerate(halves)]
    arrived = {k: swap_rows(sent[k], k * y_count) for k in others(z_count)}
    strips = [arrived[k] for k in others(z_count)]
    strips = [arrived[k] for k in others(z_count)]
    mark = guard(strips, STRIPS_FLOPS)
    blocks = [*sent, *strips, from_core, *halves]
    have, order, bit = [labels], [0], z_count // 2
    while bit:
        whole = have[0] if len(have) == 1 else join(have, PAIR_FLOPS)
        have = [whole, swap_rows(whole, bit * y_count)]
        order = order + [k ^ bit for k in order]
        bit //= 2
    base = call(
        seed_kernel,
        jax.ShapeDtypeStruct((width, classes), jnp.float32),
        seed_class.reshape(1, width),
        seed_mask.reshape(1, width),
    )

    current, scale = labels, None
    for step in range(ITERS):
        if step > 0:
            order = [0] + others_late(z_count)
            have = [current] + [swap_rows(current, k * y_count) for k in order[1:]]
        first = step == 0
        have = [join(have)] if first else [join(have[:-1]), join(have[-1:], LAST_FLOPS)]
        extra = SUBLANES if first else 0
        part = jax.ShapeDtypeStruct((width + extra, classes), jnp.float32)
        send = jax.ShapeDtypeStruct((width + 2 * extra, classes), jnp.bfloat16)
        parts = call(
            lambda *refs: ours_kernel(order, y_count, first, *refs),
            [part] * y_count,
            *blocks,
            *have,
            *([mark] if first else []),
            flops=OURS_FLOPS if first else 0,
        )
        have = [swap_cores(x) for x in have]
        wanted = range(1, y_count)
        sends = call(
            lambda *refs: theirs_kernel(order, y_count, wanted, first, *refs), [send] * (y_count - 1), *blocks, *have, *parts[1:]
        )
        (total,) = call(lambda *refs: theirs_kernel(order, y_count, [0], first, *refs), [part], *blocks, *have, parts[0])
        sends = [swap_rows(x, j + 1).astype(jnp.float32) for j, x in enumerate(sends)]
        spread = sum((x[:width] for x in sends), total[:width])
        if first:
            sums = sum((x[width : width + 3, :width].sum(axis=0) for x in sends), total[width, :width])
            scale = (CARRY / (1.0 + 0.5 * sums))[:, None]
        mixed = (0.5 * spread + current.astype(jnp.float32)) * scale
        current = (mixed + base).astype(jnp.bfloat16)
    return current


def solution(mesh):
    return jax.shard_map(
        on_device,
        mesh=mesh,
        in_specs=(
            P(("groups", "col"), None, "row"),
            P(("groups", "col"), None, "row"),
            P(("groups", "col", "row"), None),
            P(("groups", "col", "row")),
            P(("groups", "col", "row")),
        ),
        out_specs=P(("groups", "col", "row"), None),
        check_vma=False,
    )
```
